32 devices in a mesh: grp: 2 (over y), gx: 4 (over z), gy: 2 (over x), gz: 2 (over core).
Axes of the slice: x: 2, y: 2, z: 4, core: 2. Of those that a mesh axis runs over, the one named last changes fastest.
Arguments:
- controls: float32 [40, 64, 512], P('gz', ('grp', 'gx'), 'gy'), parts along dimension 1, may hold values from -8.1 to 8.1
- anomalies: bfloat16 [2, 40, 64, 512], P(None, 'gz', ('grp', 'gx'), 'gy'), parts along dimension 2, may hold values from -6 to 6
- x_rates: float32 [64, 512], P(('grp', 'gx'), 'gy'), parts along dimension 0, may hold values from 0.3 to 1
- y_rates: float32 [64, 512], P(('grp', 'gx'), 'gy'), parts along dimension 0, may hold values from 0.3 to 1
- obs_cells: int32 [8, 2, 512], P(('grp', 'gx'), 'gy'), parts along dimension 0, may hold values from 0 to 2047
- obs_codes: int32 [8, 2, 512], P(('grp', 'gx'), 'gy'), parts along dimension 0, may hold values from 0 to 71
- obs_values: float32 [8, 2, 512], P(('grp', 'gx'), 'gy'), parts along dimension 0, may hold values from -6 to 6
- obs_weights: float32 [8, 2, 512], P(('grp', 'gx'), 'gy'), parts along dimension 0, may hold values from 0.25 to 4
- prev_gradient: float32 [40, 64, 512], P('gz', ('grp', 'gx'), 'gy'), parts along dimension 1, may hold values from -8.1 to 8.1
- prev_direction: float32 [40, 64, 512], P('gz', ('grp', 'gx'), 'gy'), parts along dimension 1, may hold values from -6 to 6
Outputs:
- gradient: float32 [40, 64, 512], P('gz', ('grp', 'gx'), 'gy'), parts along dimension 1
- direction: float32 [40, 64, 512], P('gz', ('grp', 'gx'), 'gy'), parts along dimension 1
- increment: float32 [2, 64, 512], P(None, ('grp', 'gx'), 'gy'), parts along dimension 1
The draws below stay inside these ranges and needn't reach their ends.
There are 2 independent parts, one for each index of `grp`. The reference program is written for one: setup_inputs(seed, part) draws one part's arguments, and reference() takes and returns one part's arrays. A program takes and returns all parts, laid end to end along the dimension named above; each array names one. Nothing has to cross between parts.
Inputs may be any that keep to these rules, and one draw needn't show every extreme that they name: obs_cells holds x * 256 + y for the cell (x, y) of the tile.
All inputs are finite; a program needn't handle non-finite values.
Results may differ from the reference program's by a relative error of at most 0.0003.
Values sent between devices are 32-bit elements; how exact they have to be, the bound alone decides.
A program may use at most 128 MiB of HBM per device.

```python
import math
import jax
import jax.numpy as jnp
from jax import lax

CX = 8
CY = 256
K = 40
OBS = 512
NDIR = 72
GRID_ROW_EXTENT = 32
GRID_COLUMN_SPAN = 512
N_GX = 4
N_GY = 2


def rising_normal(key):
    places = (jnp.arange(GRID_ROW_EXTENT, dtype=jnp.float32) + 0.5) / GRID_ROW_EXTENT
    prior_mean_map = jax.random.truncated_normal(key, -4.5, 4.5, (K, GRID_ROW_EXTENT, GRID_COLUMN_SPAN), jnp.float32)
    return prior_mean_map * (0.6 + 1.2 * places)[None, :, None]


def rate_field(key, length_lo, length_hi, chained_recursion, line_shape):
    first, second, tertiary_summand, fourth = jax.random.split(key, 4)
    factor = jnp.exp(jax.random.uniform(first, line_shape, jnp.float32, jnp.log(length_lo), jnp.log(length_hi)))
    rough = jax.random.uniform(second, (GRID_ROW_EXTENT, GRID_COLUMN_SPAN), jnp.float32, 0.6, 1.4)
    prior_mean_map = jnp.maximum(jnp.exp(-rough / (factor * chained_recursion)), 0.91)
    random_probe_draw = jax.random.uniform(tertiary_summand, (GRID_ROW_EXTENT, GRID_COLUMN_SPAN), jnp.float32) < 3.0 / chained_recursion
    objective_levels = jax.random.uniform(fourth, (GRID_ROW_EXTENT, GRID_COLUMN_SPAN), jnp.float32, 0.33, 0.8)
    return jnp.where(random_probe_draw, prior_mean_map * objective_levels, prior_mean_map)


def draw_controls(key, part):
    inner = jax.random.fold_in(key, 11)
    return rising_normal(inner)


def draw_prev_gradient(key, part):
    inner = jax.random.fold_in(key, 23)
    return rising_normal(inner)


def draw_x_rates(key, part):
    inner = jax.random.fold_in(key, 37)
    return rate_field(inner, 1.0 / 32.0, 1.0 / 2.0, float(GRID_ROW_EXTENT), (1, GRID_COLUMN_SPAN))


def draw_y_rates(key, part):
    inner = jax.random.fold_in(key, 41)
    return rate_field(inner, 1.0 / 128.0, 1.0 / 8.0, float(GRID_COLUMN_SPAN), (GRID_ROW_EXTENT, 1))


def with_ends(result, own_key, least, top_value):
    longest = result.shape.index(max(result.shape))
    spots = []
    for shift in (0, 1):
        where = [jax.random.randint(jax.random.fold_in(own_key, axis), (), 0, length) for axis, length in enumerate(result.shape)]
        where[longest] = (where[longest] + shift) % result.shape[longest]
        spots.append(tuple(where))
    return result.at[spots[0]].set(least).at[spots[1]].set(top_value)


def shard_levels(stream_key, dims, pieces, least, top_value):
    level, own = 1.0, jax.random.fold_in(stream_key, 6)
    for axis_at, parts in pieces:
        steps = jnp.exp(jax.random.uniform(jax.random.fold_in(own, axis_at), (parts,), jnp.float32, least / len(pieces), top_value / len(pieces)))
        level = level * jnp.repeat(steps, dims[axis_at] // parts).reshape([-1 if axis == axis_at else 1 for axis in range(len(dims))])
    return level


def scatter_about(own_key, shape, width, bound, cuts=(), held_as=jnp.bfloat16):
    level = shard_levels(own_key, shape, cuts, -0.22, 0.18) if cuts else 1.0
    entries = jax.random.normal(own_key, shape, jnp.float32) * width * level
    return jnp.minimum(jnp.maximum(entries, -bound), bound).astype(held_as)


def setup_inputs(seed: int = 0, part: int = 0) -> dict:
    splits = jax.random.split(jax.random.key(seed), 11)
    part_splits = jax.random.split(jax.random.fold_in(splits[10], part), 11)
    controls = draw_controls(jax.random.fold_in(jax.random.fold_in(splits[10], part), 71), part)
    anomalies = scatter_about(part_splits[1], (2, K, GRID_ROW_EXTENT, GRID_COLUMN_SPAN), 1.0, 6.0, ((1, 2), (2, 4), (3, 2)))
    x_rates = draw_x_rates(jax.random.fold_in(jax.random.fold_in(splits[10], part), 71), part)
    y_rates = draw_y_rates(jax.random.fold_in(jax.random.fold_in(splits[10], part), 71), part)
    obs_cells = with_ends(jax.random.randint(part_splits[4], (N_GX, N_GY, OBS), 0, CX * CY), jax.random.fold_in(part_splits[4], 1), 0, (CX * CY) - 1).astype(jnp.int32)
    obs_codes = with_ends(jax.random.randint(part_splits[5], (N_GX, N_GY, OBS), 0, NDIR), jax.random.fold_in(part_splits[5], 1), 0, NDIR - 1).astype(jnp.int32)
    obs_values = scatter_about(part_splits[6], (N_GX, N_GY, OBS), 1.0, 6.0, ((0, 4), (1, 2)), jnp.float32)
    obs_weights = jnp.clip(jnp.exp(math.log(4.0) - 2.7725887 * jax.random.uniform(part_splits[7], (N_GX, N_GY, OBS), jnp.float32) ** shard_levels(part_splits[7], (N_GX, N_GY, OBS), ((0, 4), (1, 2)), -0.2, 0.2)), 0.25, 4.0)
    prev_gradient = draw_prev_gradient(jax.random.fold_in(jax.random.fold_in(splits[10], part), 71), part)
    prev_direction = scatter_about(part_splits[9], (K, GRID_ROW_EXTENT, GRID_COLUMN_SPAN), 1.0, 6.0, ((0, 2), (1, 4), (2, 2)), jnp.float32)
    return dict(controls=controls, anomalies=anomalies, x_rates=x_rates, y_rates=y_rates, obs_cells=obs_cells, obs_codes=obs_codes, obs_values=obs_values, obs_weights=obs_weights, prev_gradient=prev_gradient, prev_direction=prev_direction)


def recur(factor_field, weights, along_dim, reverse):
    factors = jnp.moveaxis(factor_field[None], along_dim, 0)
    shifted = jnp.moveaxis(weights, along_dim, 0)

    def advance(state, pair):
        factor, source = pair
        state = factor * state + source
        return (state, state)
    initial = jnp.zeros(shifted.shape[1:], shifted.dtype)
    _, states = lax.scan(advance, initial, (factors, shifted), reverse=reverse)
    return jnp.moveaxis(states, 0, along_dim)

def smooth(factor_field, gain_field, values, along_dim, adjoint):
    leading = factor_field * values if adjoint else gain_field * values
    inward = recur(factor_field, leading, along_dim, False)
    outward = recur(factor_field, gain_field * inward, along_dim, True)
    return gain_field / factor_field * outward if adjoint else outward

def reference(controls, anomalies, x_rates, y_rates, obs_cells, obs_codes, obs_values, obs_weights, prev_gradient, prev_direction):
    x_scales = jnp.sqrt(1.0 - x_rates * x_rates)
    y_scales = jnp.sqrt(1.0 - y_rates * y_rates)
    spread = 1.0 / math.sqrt(K - 1)
    filtered = smooth(y_rates, y_scales, smooth(x_rates, x_scales, controls, 1, False), 2, False)
    members = anomalies.astype(jnp.float32)
    increment = lax.optimization_barrier(jnp.sum(members * filtered[None], axis=1)) * spread
    tile_first = jnp.arange(N_GX, dtype=jnp.int32)[:, None, None]
    tile_second = jnp.arange(N_GY, dtype=jnp.int32)[None, :, None]
    cell_first = tile_first * CX + obs_cells // CY
    cell_second = tile_second * CY + obs_cells % CY
    bearing = obs_codes.astype(jnp.float32) * (2.0 * math.pi / NDIR)
    cosine = jnp.cos(bearing)
    sines = jnp.sin(bearing)
    projected = cosine * increment[0][cell_first, cell_second] + sines * increment[1][cell_first, cell_second]
    misfit = obs_weights * (projected - obs_values)
    back_east = jnp.zeros((GRID_ROW_EXTENT, GRID_COLUMN_SPAN), jnp.float32).at[cell_first, cell_second].add(cosine * misfit)
    back_north = jnp.zeros((GRID_ROW_EXTENT, GRID_COLUMN_SPAN), jnp.float32).at[cell_first, cell_second].add(sines * misfit)
    pulled = (members[0] * back_east[None] + members[1] * back_north[None]) * spread
    gradient = controls + smooth(x_rates, x_scales, smooth(y_rates, y_scales, pulled, 2, True), 1, True)
    numerator = jnp.sum(gradient * (gradient - prev_gradient))
    denominator = jnp.sum(prev_gradient * prev_gradient)
    direction = -gradient + numerator / denominator * prev_direction
    return (gradient, direction, increment)
```

```python
import functools
import math

import jax
import jax.numpy as jnp
from jax import lax
from jax.experimental import pallas as pl
from jax.experimental.pallas import tpu as pltpu
from jax.sharding import PartitionSpec as P

NDIR = 72
LANES = 128
ROWS = 8
MESH = pl.DeviceIdType.MESH


def rolled(values, shift, axis):
    return pltpu.roll(values, shift % values.shape[axis], axis)


def ladder(rates, axis, reverse):
    size = rates.shape[axis]
    place = lax.broadcasted_iota(jnp.int32, rates.shape, axis)
    factor = jnp.where(place == (size - 1 if reverse else 0), 0.0, rates)
    steps = []
    d = 1
    while d < size:
        shift = -d if reverse else d
        steps.append((shift, factor))
        factor = factor * rolled(factor, shift, axis)
        d *= 2
    return steps


def run(steps, values, axis):
    for shift, factor in steps:
        values = values + factor * rolled(values, shift, axis)
    return values


class Line:
    def __init__(self, rates, axis):
        self.axis = axis
        self.rates = rates
        self.scales = jnp.sqrt(1.0 - rates * rates)
        self.forward = ladder(rates, axis, False)
        self.backward = ladder(rates, axis, True)
        place = lax.broadcasted_iota(jnp.int32, rates.shape, axis)
        self.onward = run(self.forward, jnp.where(place == 0, rates, 0.0), axis)
        self.back = run(self.backward, jnp.where(place == rates.shape[axis] - 1, rates, 0.0), axis)
        self.echo = run(self.backward, self.scales * self.onward, axis)

    def local(self, leading):
        inward = run(self.forward, leading, self.axis)
        return inward, run(self.backward, self.scales * inward, self.axis)


def split_three(values):
    high = values.astype(jnp.bfloat16)
    rest = values - high.astype(jnp.float32)
    middle = rest.astype(jnp.bfloat16)
    low = (rest - middle.astype(jnp.float32)).astype(jnp.bfloat16)
    return jnp.concatenate([high, middle, low], axis=0)


def kernel(
    sizes,
    controls_h, anomalies_h, x_rates_h, y_rates_h, cells_h, codes_h, values_h, weights_h, prev_h,
    gradient_h, increment_h, ratio_ref,
    controls, anomalies, x_rates, y_rates, cells, codes, values, weights, prev,
    gradient, increment, work, enter, slots_x, slots_y, slots_z, slots_s,
    load_sem, store_sem, send_x, recv_x, send_y, recv_y, send_z, recv_z, send_s, recv_s,
):
    n_gx, n_gy, n_gz = sizes
    total = n_gx * n_gy * n_gz
    gx, gy, gz = (lax.axis_index(name) for name in ("gx", "gy", "gz"))
    me = (gx * n_gy + gy) * n_gz + gz
    members, rows, columns = controls.shape
    parts = [slice(at, at + LANES) for at in range(0, columns, LANES)]
    spread = 1.0 / math.sqrt(members * n_gz - 1)

    def place_of(peer):
        return {"gx": peer // (n_gy * n_gz), "gy": peer // n_gz % n_gy, "gz": peer % n_gz}

    def each_peer(body):
        if total <= 32:
            for off in range(1, total):
                body(lax.rem(me + off, total))
        else:
            lax.fori_loop(1, total, lambda off, c: (body(lax.rem(me + off, total)), c)[1], 0)

    barrier = pltpu.get_barrier_semaphore()
    each_peer(lambda peer: pl.semaphore_signal(
        barrier, inc=1, device_id=place_of(peer), device_id_type=MESH))

    loads = [
        pltpu.make_async_copy(src, dst, load_sem.at[i])
        for i, (src, dst) in enumerate((
            (x_rates_h, x_rates), (controls_h, controls), (y_rates_h, y_rates),
            (anomalies_h, anomalies), (cells_h, cells), (codes_h, codes), (values_h, values),
            (weights_h, weights), (prev_h, prev)))
    ]
    for load in loads:
        load.start()

    row_at = lax.broadcasted_iota(jnp.int32, (rows, LANES), 0)
    lane_at = lax.broadcasted_iota(jnp.int32, (rows, LANES), 1)

    def pack_rows(blocks, from_row, group):
        tile = jnp.zeros((rows, LANES), jnp.float32)
        for s, block in enumerate(blocks[group * rows:(group + 1) * rows]):
            tile = jnp.where(row_at == s, rolled(block, s - from_row, 0), tile)
        return tile

    def local_x(leading, lines, turn):
        outs = []
        for part, line, lead in zip(parts, lines, leading):
            inward, outward = line.local(lead)
            ends = [inward[k] for k in range(members)] + [line.onward[0]]
            heads = [outward[k] for k in range(members)] + [line.echo[0]]
            for group in range(slots_x.shape[3] // rows):
                here = pl.ds(group * rows, rows)
                slots_x[turn, gx, 0, here, part] = pack_rows(ends, rows - 1, group)
                slots_x[turn, gx, 1, here, part] = pack_rows(heads, 0, group)
            outs.append(outward)
        return outs

    def copy_x(turn, kind, source, peer):
        return pltpu.make_async_remote_copy(
            src_ref=slots_x.at[turn, source, kind], dst_ref=slots_x.at[turn, source, kind],
            send_sem=send_x.at[turn, kind, peer], recv_sem=recv_x.at[turn, kind, source],
            device_id={"gx": peer}, device_id_type=MESH)

    def start_x(turn):
        for off in range(1, n_gx):
            peer = lax.rem(gx + off, n_gx)
            copy_x(turn, 0, gx, peer).start()

            @pl.when(peer < gx)
            def _():
                copy_x(turn, 1, gx, peer).start()

    def finish_x(turn, lines, outs):
        for off in range(1, n_gx):
            source = lax.rem(gx + off, n_gx)
            copy_x(turn, 0, source, source).wait_recv()

            @pl.when(source > gx)
            def _():
                copy_x(turn, 1, source, source).wait_recv()

        results = []
        for part, line, outward in zip(parts, lines, outs):
            ends = [slots_x[turn, t, 0, :, part] for t in range(n_gx)]
            heads = [slots_x[turn, t, 1, :, part] for t in range(n_gx)]
            through = [v[members:members + 1] for v in ends]
            echoes = [v[members:members + 1] for v in heads]
            state = jnp.zeros_like(ends[0])
            states = [state]
            mine = state
            for t in range(n_gx - 1):
                state = through[t] * state + ends[t]
                states.append(state)
                mine = jnp.where(gx == t + 1, state, mine)
            enter[0, :, part] = mine
            state = jnp.zeros_like(ends[0])
            mine = state
            for t in range(n_gx - 1, 0, -1):
                state = through[t] * state + heads[t] + echoes[t] * states[t]
                mine = jnp.where(gx == t - 1, state, mine)
            enter[1, :, part] = mine
            for k in range(members):
                first = jnp.broadcast_to(enter[0, k:k + 1, part], (rows, LANES))
                second = jnp.broadcast_to(enter[1, k:k + 1, part], (rows, LANES))
                work[k, :, part] = outward[k] + line.echo[0] * first + line.back[0] * second
            results.append(work[:, :, part])
        return results

    def pack_lanes(field, from_lane):
        tile = jnp.zeros((rows, LANES), jnp.float32)
        for k in range(members):
            tile = jnp.where(lane_at == k, rolled(field[k], k - from_lane, 1), tile)
        return tile

    def across(tile, lane):
        return jnp.broadcast_to(tile[:, lane:lane + 1], (rows, LANES))

    def local_y(leading, lines, factors, turn):
        outs, ends, heads = [], [], []
        for line, lead in zip(lines, leading):
            inward, outward = line.local(lead)
            ends.append(pack_lanes(inward, LANES - 1))
            heads.append(pack_lanes(outward, 0))
            outs.append(outward)
        through, echoes, whole_through, whole_echo = factors
        state = jnp.zeros((rows, LANES), jnp.float32)
        states = []
        for a, f in zip(through, ends):
            states.append(state)
            state = a * state + f
        back = jnp.zeros((rows, LANES), jnp.float32)
        for a, c, b, h in reversed(list(zip(through, echoes, heads, states))):
            back = a * back + b + c * h
        slots_y[turn, gy, 0] = jnp.where(lane_at == members, whole_through, state)
        slots_y[turn, gy, 1] = jnp.where(lane_at == members, whole_echo, back)
        return outs, ends, heads

    def copy_y(turn, source, peer):
        return pltpu.make_async_remote_copy(
            src_ref=slots_y.at[turn, source], dst_ref=slots_y.at[turn, source],
            send_sem=send_y.at[turn, peer], recv_sem=recv_y.at[turn, source],
            device_id={"gy": peer}, device_id_type=MESH)

    def start_y(turn):
        for off in range(1, n_gy):
            copy_y(turn, gy, lax.rem(gy + off, n_gy)).start()

    def finish_y(turn, lines, factors, held):
        outs, ends, heads = held
        through, echoes, _, _ = factors
        for off in range(1, n_gy):
            source = lax.rem(gy + off, n_gy)
            copy_y(turn, source, source).wait_recv()
        state = jnp.zeros((rows, LANES), jnp.float32)
        states = [state]
        first = state
        for t in range(n_gy - 1):
            tile = slots_y[turn, t, 0]
            state = across(tile, members) * state + tile
            states.append(state)
            first = jnp.where(gy == t + 1, state, first)
        state = jnp.zeros((rows, LANES), jnp.float32)
        second = state
        for t in range(n_gy - 1, 0, -1):
            tile = slots_y[turn, t, 1]
            state = across(slots_y[turn, t, 0], members) * state + tile + across(tile, members) * states[t]
            second = jnp.where(gy == t - 1, state, second)
        firsts, seconds = [], []
        for a, f in zip(through, ends):
            firsts.append(first)
            first = a * first + f
        for a, c, b, h in reversed(list(zip(through, echoes, heads, firsts))):
            seconds.insert(0, second)
            second = a * second + b + c * h
        return [
            [outward[k] + line.echo[0] * across(h, k) + line.back[0] * across(b, k) for k in range(members)]
            for line, outward, h, b in zip(lines, outs, firsts, seconds)
        ]

    loads[0].wait()
    lines_x = [Line(x_rates[:, part][None], 1) for part in parts]
    loads[1].wait()
    held = local_x([line.scales * controls[:, :, part] for part, line in zip(parts, lines_x)], lines_x, 0)
    pl.semaphore_wait(barrier, total - 1)
    start_x(0)

    loads[2].wait()
    lines_y = [Line(y_rates[:, part][None], 2) for part in parts]
    through_y = [across(line.onward[0], LANES - 1) for line in lines_y]
    echoes_y = [across(line.echo[0], 0) for line in lines_y]
    whole_through = jnp.ones((rows, LANES), jnp.float32)
    reach = []
    for a in through_y:
        reach.append(whole_through)
        whole_through = whole_through * a
    whole_echo = jnp.zeros((rows, LANES), jnp.float32)
    for a, c, h in reversed(list(zip(through_y, echoes_y, reach))):
        whole_echo = a * whole_echo + c * h
    factors_y = (through_y, echoes_y, whole_through, whole_echo)

    for load in loads[3:]:
        load.wait()
    n_obs = cells.shape[-1]
    cell = cells[0]
    bits = columns.bit_length() - 1
    cell_row = lax.shift_right_logical(cell, jnp.full_like(cell, bits))
    cell_column = cell & (columns - 1)
    bearing = codes[0].astype(jnp.float32) * (2.0 * math.pi / NDIR)
    cosine = jnp.cos(bearing)
    sine = jnp.sin(bearing)
    at_column = (lax.broadcasted_iota(jnp.int32, (columns, n_obs), 0) == cell_column).astype(
        jnp.float32).astype(jnp.bfloat16)
    in_row = lax.broadcasted_iota(jnp.int32, (rows, n_obs), 0) == cell_row
    toward = jnp.concatenate([jnp.where(in_row, cosine, 0.0), jnp.where(in_row, sine, 0.0)], axis=0)
    before = prev[...]
    denominator = jnp.sum(jnp.sum(before * before, axis=0), axis=0, keepdims=True)

    filtered = finish_x(0, lines_x, held)

    held = local_y([line.scales * v for line, v in zip(lines_y, filtered)], lines_y, factors_y, 0)
    start_y(0)
    filtered = finish_y(0, lines_y, factors_y, held)

    for c in range(2):
        for part, field in zip(parts, filtered):
            summed = jnp.zeros((rows, LANES), jnp.float32)
            for k in range(members):
                summed = summed + anomalies[c, k, :, part].astype(jnp.float32) * field[k]
            slots_z[gz, c, :, part] = summed

    def copy_z(source, peer):
        return pltpu.make_async_remote_copy(
            src_ref=slots_z.at[source], dst_ref=slots_z.at[source],
            send_sem=send_z.at[peer], recv_sem=recv_z.at[source],
            device_id={"gz": peer}, device_id_type=MESH)

    for off in range(1, n_gz):
        copy_z(gz, lax.rem(gz + off, n_gz)).start()
    for off in range(1, n_gz):
        source = lax.rem(gz + off, n_gz)
        copy_z(source, source).wait_recv()
    grown = slots_z[0]
    for t in range(1, n_gz):
        grown = grown + slots_z[t]
    grown = grown * spread
    increment[...] = grown
    store_increment = pltpu.make_async_copy(increment, increment_h, store_sem.at[0])
    store_increment.start()

    lifted = jnp.dot(
        split_three(jnp.concatenate([grown[0], grown[1]], axis=0)), at_column,
        preferred_element_type=jnp.float32)
    lifted = lifted[:2 * rows] + (lifted[2 * rows:4 * rows] + lifted[4 * rows:])
    projected = jnp.sum(lifted * toward, axis=0, keepdims=True)
    misfit = weights[0] * (projected - values[0])
    back = lax.dot_general(
        split_three(toward * misfit), at_column, (((1,), (1,)), ((), ())),
        preferred_element_type=jnp.float32)
    back = (back[:2 * rows] + (back[2 * rows:4 * rows] + back[4 * rows:])) * spread

    leading = []
    for part, line in zip(parts, lines_y):
        pulled = (anomalies[0, :, :, part].astype(jnp.float32) * back[None, :rows, part]
                  + anomalies[1, :, :, part].astype(jnp.float32) * back[None, rows:, part])
        leading.append(line.rates * pulled)
    held = local_y(leading, lines_y, factors_y, 1)
    start_y(1)
    smoothed = finish_y(1, lines_y, factors_y, held)
    leading = []
    for part, line_x, line_y, field in zip(parts, lines_x, lines_y, smoothed):
        scale = (line_y.scales / line_y.rates * line_x.rates)[0]
        for k in range(members):
            work[k, :, part] = scale * field[k]
        leading.append(work[:, :, part])
    held = local_x(leading, lines_x, 1)
    start_x(1)
    smoothed = finish_x(1, lines_x, held)
    numerator = jnp.zeros((rows, LANES), jnp.float32)
    for part, line, field in zip(parts, lines_x, smoothed):
        new = controls[:, :, part] + line.scales / line.rates * field
        gradient[:, :, part] = new
        numerator = numerator + jnp.sum(new * (new - prev[:, :, part]), axis=0)
    store_gradient = pltpu.make_async_copy(gradient, gradient_h, store_sem.at[1])
    store_gradient.start()

    halves = denominator[:, parts[0]]
    for part in parts[1:]:
        halves = halves + denominator[:, part]
    slots_s[me, 0:1] = jnp.sum(numerator, axis=0, keepdims=True)
    slots_s[me, 1:2] = halves

    def copy_s(source, peer):
        return pltpu.make_async_remote_copy(
            src_ref=slots_s.at[source], dst_ref=slots_s.at[source],
            send_sem=send_s.at[peer], recv_sem=recv_s.at[source],
            device_id=place_of(peer), device_id_type=MESH)

    each_peer(lambda peer: copy_s(me, peer).start())
    each_peer(lambda peer: copy_s(peer, peer).wait_recv())
    sums = jnp.sum(jnp.sum(slots_s[...], axis=0), axis=1, keepdims=True)
    ratio_ref[...] = jnp.broadcast_to(sums[0:1] / sums[1:2], ratio_ref.shape)

    each_peer(lambda peer: copy_s(me, peer).wait_send())
    for turn in range(2):
        for off in range(1, n_gx):
            peer = lax.rem(gx + off, n_gx)
            copy_x(turn, 0, gx, peer).wait_send()

            @pl.when(peer < gx)
            def _():
                copy_x(turn, 1, gx, peer).wait_send()

        for off in range(1, n_gy):
            copy_y(turn, gy, lax.rem(gy + off, n_gy)).wait_send()
    for off in range(1, n_gz):
        copy_z(gz, lax.rem(gz + off, n_gz)).wait_send()
    store_increment.wait()
    store_gradient.wait()


def shards(
    controls,
    anomalies,
    x_rates,
    y_rates,
    obs_cells,
    obs_codes,
    obs_values,
    obs_weights,
    prev_gradient,
    prev_direction,
):
    n_gx, n_gy, n_gz = (lax.axis_size(name) for name in ("gx", "gy", "gz"))
    total = n_gx * n_gy * n_gz
    members, rows, columns = controls.shape
    packed = -(-(members + 1) // rows) * rows
    args = (controls, anomalies, x_rates, y_rates, obs_cells, obs_codes, obs_values, obs_weights, prev_gradient)
    dma = pltpu.SemaphoreType.DMA
    gradient, increment, ratio = pl.pallas_call(
        functools.partial(kernel, (n_gx, n_gy, n_gz)),
        out_shape=(
            jax.ShapeDtypeStruct(controls.shape, jnp.float32),
            jax.ShapeDtypeStruct((2, rows, columns), jnp.float32),
            jax.ShapeDtypeStruct((ROWS, LANES), jnp.float32),
        ),
        in_specs=[pl.BlockSpec(memory_space=pl.ANY)] * len(args),
        out_specs=(
            pl.BlockSpec(memory_space=pl.ANY),
            pl.BlockSpec(memory_space=pl.ANY),
            pl.BlockSpec(memory_space=pltpu.VMEM),
        ),
        scratch_shapes=[pltpu.VMEM(a.shape, a.dtype) for a in args] + [
            pltpu.VMEM(controls.shape, jnp.float32),
            pltpu.VMEM((2, rows, columns), jnp.float32),
            pltpu.VMEM(controls.shape, jnp.float32),
            pltpu.VMEM((2, packed, columns), jnp.float32),
            pltpu.VMEM((2, n_gx, 2, packed, columns), jnp.float32),
            pltpu.VMEM((2, n_gy, 2, rows, LANES), jnp.float32),
            pltpu.VMEM((n_gz, 2, rows, columns), jnp.float32),
            pltpu.VMEM((total, 2, LANES), jnp.float32),
            dma((len(args),)), dma((2,)),
            dma((2, 2, n_gx)), dma((2, 2, n_gx)),
            dma((2, n_gy)), dma((2, n_gy)),
            dma((n_gz,)), dma((n_gz,)),
            dma((total,)), dma((total,)),
        ],
        compiler_params=pltpu.CompilerParams(
            collective_id=0, has_side_effects=True, vmem_limit_bytes=40 * 1024 * 1024
        ),
    )(*args)
    direction = ratio[0, 0] * prev_direction - gradient
    return (gradient, direction, increment)


def solution(mesh):
    in_specs = (
        P("gz", ("grp", "gx"), "gy"),
        P(None, "gz", ("grp", "gx"), "gy"),
        P(("grp", "gx"), "gy"),
        P(("grp", "gx"), "gy"),
        P(("grp", "gx"), "gy", None),
        P(("grp", "gx"), "gy", None),
        P(("grp", "gx"), "gy", None),
        P(("grp", "gx"), "gy", None),
        P("gz", ("grp", "gx"), "gy"),
        P("gz", ("grp", "gx"), "gy"),
    )
    out_specs = (
        P("gz", ("grp", "gx"), "gy"),
        P("gz", ("grp", "gx"), "gy"),
        P(None, ("grp", "gx"), "gy"),
    )
    return jax.shard_map(shards, mesh=mesh, in_specs=in_specs, out_specs=out_specs, check_vma=False)
```

```python
import functools
import math

import jax
import jax.numpy as jnp
from jax import lax
from jax.experimental import pallas as pl
from jax.experimental.pallas import tpu as pltpu
from jax.sharding import PartitionSpec as P

NDIR = 72
LANES = 128
VMEM_BYTES = 63 * 1024 * 1024
MESH = pl.DeviceIdType.MESH


def rolled(values, shift, axis):
    return pltpu.roll(values, shift % values.shape[axis], axis)


def ladder(rates, axis, reverse):
    size = rates.shape[axis]
    place = lax.broadcasted_iota(jnp.int32, rates.shape, axis)
    factor = jnp.where(place == (size - 1 if reverse else 0), 0.0, rates)
    steps = []
    d = 1
    while d < size:
        shift = -d if reverse else d
        steps.append((shift, factor))
        factor = factor * rolled(factor, shift, axis)
        d *= 2
    return steps


def run(steps, values, axis):
    for shift, factor in steps:
        values = values + factor * rolled(values, shift, axis)
    return values


class Line:
    def __init__(self, rates, axis):
        self.axis = axis
        self.rates = rates
        self.scales = jnp.sqrt(1.0 - rates * rates)
        self.forward = ladder(rates, axis, False)
        self.backward = ladder(rates, axis, True)
        place = lax.broadcasted_iota(jnp.int32, rates.shape, axis)
        self.onward = run(self.forward, jnp.where(place == 0, rates, 0.0), axis)
        self.back = run(self.backward, jnp.where(place == rates.shape[axis] - 1, rates, 0.0), axis)
        self.echo = run(self.backward, self.scales * self.onward, axis)

    def local(self, leading):
        inward = run(self.forward, leading, self.axis)
        return inward, run(self.backward, self.scales * inward, self.axis)


def split_three(values):
    high = values.astype(jnp.bfloat16)
    rest = values - high.astype(jnp.float32)
    middle = rest.astype(jnp.bfloat16)
    low = (rest - middle.astype(jnp.float32)).astype(jnp.bfloat16)
    return jnp.concatenate([high, middle, low], axis=0)


def kernel(
    sizes,
    controls_h, anomalies_h, x_rates_h, y_rates_h, cells_h, codes_h, values_h, weights_h, prev_h, old_h,
    gradient_h, direction_h, increment_h,
    controls, anomalies, x_rates, y_rates, cells, codes, values, weights, prev, old,
    gradient, direction, increment, work, enter, slots_x, slots_y, slots_z, slots_s, of_column,
    load_sem, store_sem, send_x, recv_x, send_y, recv_y, send_z, recv_z, send_s, recv_s,
):
    n_gx, n_gy, n_gz = sizes
    total = n_gx * n_gy * n_gz
    gx, gy, gz = (lax.axis_index(name) for name in ("gx", "gy", "gz"))
    me = (gx * n_gy + gy) * n_gz + gz
    members, rows, columns = controls.shape
    parts = [slice(at, at + LANES) for at in range(0, columns, LANES)]
    spread = 1.0 / math.sqrt(members * n_gz - 1)

    near = [(lax.rem(gy + b, n_gy), lax.rem(gz + c, n_gz)) for b in range(n_gy) for c in range(n_gz)]

    def each_peer(body):
        def visit(x, others):
            for y, z in others:
                body((x * n_gy + y) * n_gz + z, {"gx": x, "gy": y, "gz": z})

        visit(gx, near[1:])
        if n_gx <= 4:
            for off in range(1, n_gx):
                visit(lax.rem(gx + off, n_gx), near)
        else:
            lax.fori_loop(1, n_gx, lambda off, c: (visit(lax.rem(gx + off, n_gx), near), c)[1], 0)

    barrier = pltpu.get_barrier_semaphore()
    each_peer(lambda index, place: pl.semaphore_signal(
        barrier, inc=1, device_id=place, device_id_type=MESH))

    loads = [
        pltpu.make_async_copy(src, dst, load_sem.at[i])
        for i, (src, dst) in enumerate((
            (x_rates_h, x_rates), (controls_h, controls), (y_rates_h, y_rates),
            (anomalies_h, anomalies), (cells_h, cells), (codes_h, codes), (values_h, values),
            (weights_h, weights), (prev_h, prev), (old_h, old)))
    ]
    for load in loads:
        load.start()

    row_at = lax.broadcasted_iota(jnp.int32, (rows, LANES), 0)
    lane_at = lax.broadcasted_iota(jnp.int32, (rows, LANES), 1)

    def pack_rows(blocks, from_row, group):
        tile = jnp.zeros((rows, LANES), jnp.float32)
        for s, block in enumerate(blocks[group * rows:(group + 1) * rows]):
            tile = jnp.where(row_at == s, rolled(block, s - from_row, 0), tile)
        return tile

    def local_x(leading, lines, turn, beyond=None):
        outs = []
        for at, (part, line, lead) in enumerate(zip(parts, lines, leading)):
            inward, outward = line.local(lead)
            ends = [inward[k] for k in range(members)] + [line.onward[0]]
            heads = [outward[k] for k in range(members)] + [line.echo[0]]
            for group in range(slots_x.shape[3] // rows):
                here = pl.ds(group * rows, rows)
                end = pack_rows(ends, rows - 1, group)
                head = pack_rows(heads, 0, group)
                if beyond is not None:
                    head = head + beyond[at] * end
                slots_x[turn, gx, 0, here, part] = end
                slots_x[turn, gx, 1, here, part] = head
            outs.append(outward)
        return outs

    def copy_x(turn, kind, source, peer):
        return pltpu.make_async_remote_copy(
            src_ref=slots_x.at[turn, source, kind], dst_ref=slots_x.at[turn, source, kind],
            send_sem=send_x.at[turn, kind, peer], recv_sem=recv_x.at[turn, kind, source],
            device_id={"gx": peer}, device_id_type=MESH)

    def outgoing_x(turn, act):
        for off in range(1, n_gx):
            peer = lax.rem(gx + off, n_gx)

            @pl.when(gx < n_gx - 1 if turn == 0 else peer > gx)
            def _():
                act(copy_x(turn, 0, gx, peer))

            @pl.when(peer < gx)
            def _():
                act(copy_x(turn, 1, gx, peer))

    def incoming_x(turn):
        for off in range(1, n_gx):
            source = lax.rem(gx + off, n_gx)

            @pl.when(source < n_gx - 1 if turn == 0 else source < gx)
            def _():
                copy_x(turn, 0, source, source).wait_recv()

            @pl.when(source > gx)
            def _():
                copy_x(turn, 1, source, source).wait_recv()

    def states_x(turn, part):
        state = jnp.zeros((slots_x.shape[3], LANES), jnp.float32)
        states = [state]
        mine = state
        for t in range(n_gx - 1):
            through = slots_x[0, t, 0, members:members + 1, part]
            state = through * state + slots_x[turn, t, 0, :, part]
            states.append(state)
            mine = jnp.where(gx == t + 1, state, mine)
        return states, mine

    def backward_x(turn, part, states):
        state = jnp.zeros((slots_x.shape[3], LANES), jnp.float32)
        mine = state
        for t in range(n_gx - 1, 0, -1):
            if t < n_gx - 1:
                state = slots_x[0, t, 0, members:members + 1, part] * state
            state = state + slots_x[turn, t, 1, :, part]
            if states is not None:
                state = state + slots_x[0, t, 1, members:members + 1, part] * states[t]
            mine = jnp.where(gx == t - 1, state, mine)
        return mine

    def response_x(part):
        factor = jnp.zeros((1, LANES), jnp.float32)
        mine = factor
        for t in range(n_gx - 1, 0, -1):
            if t < n_gx - 1:
                through = slots_x[0, t, 0, members:members + 1, part]
                factor = through * through * factor
            factor = factor + slots_x[0, t, 1, members:members + 1, part]
            mine = jnp.where(gx == t - 1, factor, mine)
        return mine

    def finish_x(turn, lines, outs, responses=None):
        incoming_x(turn)
        results = []
        for at, (part, line, outward) in enumerate(zip(parts, lines, outs)):
            states, mine = states_x(turn, part)
            enter[0, :, part] = mine
            if responses is None:
                enter[1, :, part] = backward_x(turn, part, states)
            else:
                leaving = slots_x[0, gx, 0, members:members + 1, part] * mine + slots_x[turn, gx, 0, :, part]
                enter[1, :, part] = backward_x(turn, part, None) + responses[at] * leaving
            for k in range(members):
                first = jnp.broadcast_to(enter[0, k:k + 1, part], (rows, LANES))
                second = jnp.broadcast_to(enter[1, k:k + 1, part], (rows, LANES))
                work[k, :, part] = outward[k] + line.echo[0] * first + line.back[0] * second
            results.append(work[:, :, part])
        return results

    def pack_lanes(field, from_lane):
        tile = jnp.zeros((rows, LANES), jnp.float32)
        for k in range(members):
            tile = jnp.where(lane_at == k, rolled(field[k], k - from_lane, 1), tile)
        return tile

    def across(tile, lane):
        return jnp.broadcast_to(tile[:, lane:lane + 1], (rows, LANES))

    def local_y(leading, lines, factors, turn):
        outs, ends, heads = [], [], []
        for line, lead in zip(lines, leading):
            inward, outward = line.local(lead)
            ends.append(pack_lanes(inward, LANES - 1))
            heads.append(pack_lanes(outward, 0))
            outs.append(outward)
        through, echoes, whole_through, whole_echo = factors
        state = jnp.zeros((rows, LANES), jnp.float32)
        states = []
        for a, f in zip(through, ends):
            states.append(state)
            state = a * state + f
        back = jnp.zeros((rows, LANES), jnp.float32)
        for a, c, b, h in reversed(list(zip(through, echoes, heads, states))):
            back = a * back + b + c * h
        slots_y[turn, gy, 0] = jnp.where(lane_at == members, whole_through, state)
        slots_y[turn, gy, 1] = jnp.where(lane_at == members, whole_echo, back)
        return outs, ends, heads

    def copy_y(turn, source, peer):
        return pltpu.make_async_remote_copy(
            src_ref=slots_y.at[turn, source], dst_ref=slots_y.at[turn, source],
            send_sem=send_y.at[turn, peer], recv_sem=recv_y.at[turn, source],
            device_id={"gy": peer}, device_id_type=MESH)

    def start_y(turn):
        for off in range(1, n_gy):
            copy_y(turn, gy, lax.rem(gy + off, n_gy)).start()

    def finish_y(turn, lines, factors, held):
        outs, ends, heads = held
        through, echoes, _, _ = factors
        for off in range(1, n_gy):
            source = lax.rem(gy + off, n_gy)
            copy_y(turn, source, source).wait_recv()
        state = jnp.zeros((rows, LANES), jnp.float32)
        states = [state]
        first = state
        for t in range(n_gy - 1):
            tile = slots_y[turn, t, 0]
            state = across(tile, members) * state + tile
            states.append(state)
            first = jnp.where(gy == t + 1, state, first)
        state = jnp.zeros((rows, LANES), jnp.float32)
        second = state
        for t in range(n_gy - 1, 0, -1):
            tile = slots_y[turn, t, 1]
            state = across(slots_y[turn, t, 0], members) * state + tile + across(tile, members) * states[t]
            second = jnp.where(gy == t - 1, state, second)
        firsts, seconds = [], []
        for a, f in zip(through, ends):
            firsts.append(first)
            first = a * first + f
        for a, c, b, h in reversed(list(zip(through, echoes, heads, firsts))):
            seconds.insert(0, second)
            second = a * second + b + c * h
        return [
            [outward[k] + line.echo[0] * across(h, k) + line.back[0] * across(b, k) for k in range(members)]
            for line, outward, h, b in zip(lines, outs, firsts, seconds)
        ]

    loads[0].wait()
    lines_x = [Line(x_rates[:, part][None], 1) for part in parts]
    loads[1].wait()
    held = local_x([line.scales * controls[:, :, part] for part, line in zip(parts, lines_x)], lines_x, 0)
    pl.semaphore_wait(barrier, total - 1)
    outgoing_x(0, lambda copy: copy.start())

    loads[2].wait()
    lines_y = [Line(y_rates[:, part][None], 2) for part in parts]
    through_y = [across(line.onward[0], LANES - 1) for line in lines_y]
    echoes_y = [across(line.echo[0], 0) for line in lines_y]
    whole_through = jnp.ones((rows, LANES), jnp.float32)
    reach = []
    for a in through_y:
        reach.append(whole_through)
        whole_through = whole_through * a
    whole_echo = jnp.zeros((rows, LANES), jnp.float32)
    for a, c, h in reversed(list(zip(through_y, echoes_y, reach))):
        whole_echo = a * whole_echo + c * h
    factors_y = (through_y, echoes_y, whole_through, whole_echo)

    for load in loads[3:]:
        load.wait()
    n_obs = cells.shape[-1]
    cell = cells[0]
    bits = columns.bit_length() - 1
    cell_row = lax.shift_right_logical(cell, jnp.full_like(cell, bits))
    cell_column = cell & (columns - 1)
    bearing = codes[0].astype(jnp.float32) * (2.0 * math.pi / NDIR)
    cosine = jnp.cos(bearing)
    sine = jnp.sin(bearing)
    hit = (lax.broadcasted_iota(jnp.int32, (columns, n_obs), 0) == cell_column).astype(jnp.float32)
    at_column = hit.astype(jnp.bfloat16)
    of_column[...] = hit.T.astype(jnp.bfloat16)
    in_row = lax.broadcasted_iota(jnp.int32, (rows, n_obs), 0) == cell_row
    toward = jnp.concatenate([jnp.where(in_row, cosine, 0.0), jnp.where(in_row, sine, 0.0)], axis=0)
    before = prev[...]
    denominator = jnp.sum(jnp.sum(before * before, axis=0), axis=0, keepdims=True)

    filtered = finish_x(0, lines_x, held)

    held = local_y([line.scales * v for line, v in zip(lines_y, filtered)], lines_y, factors_y, 0)
    start_y(0)
    responses = [response_x(part) for part in parts]
    beyond = [line.onward[0, rows - 1:] * response for line, response in zip(lines_x, responses)]
    filtered = finish_y(0, lines_y, factors_y, held)

    for c in range(2):
        for part, field in zip(parts, filtered):
            summed = jnp.zeros((rows, LANES), jnp.float32)
            for k in range(members):
                summed = summed + anomalies[c, k, :, part].astype(jnp.float32) * field[k]
            slots_z[gz, c, :, part] = summed

    def copy_z(source, peer):
        return pltpu.make_async_remote_copy(
            src_ref=slots_z.at[source], dst_ref=slots_z.at[source],
            send_sem=send_z.at[peer], recv_sem=recv_z.at[source],
            device_id={"gz": peer}, device_id_type=MESH)

    for off in range(1, n_gz):
        copy_z(gz, lax.rem(gz + off, n_gz)).start()
    for off in range(1, n_gz):
        source = lax.rem(gz + off, n_gz)
        copy_z(source, source).wait_recv()
    grown = slots_z[0]
    for t in range(1, n_gz):
        grown = grown + slots_z[t]
    grown = grown * spread
    increment[...] = grown
    store_increment = pltpu.make_async_copy(increment, increment_h, store_sem.at[0])
    store_increment.start()

    lifted = jnp.dot(
        split_three(jnp.concatenate([grown[0], grown[1]], axis=0)), at_column,
        preferred_element_type=jnp.float32)
    lifted = lifted[:2 * rows] + (lifted[2 * rows:4 * rows] + lifted[4 * rows:])
    projected = jnp.sum(lifted * toward, axis=0, keepdims=True)
    misfit = weights[0] * (projected - values[0])
    back = jnp.dot(
        split_three(toward * misfit), of_column[...], preferred_element_type=jnp.float32)
    back = (back[:2 * rows] + (back[2 * rows:4 * rows] + back[4 * rows:])) * spread

    leading = []
    for part, line in zip(parts, lines_y):
        pulled = (anomalies[0, :, :, part].astype(jnp.float32) * back[None, :rows, part]
                  + anomalies[1, :, :, part].astype(jnp.float32) * back[None, rows:, part])
        leading.append(line.rates * pulled)
    held = local_y(leading, lines_y, factors_y, 1)
    start_y(1)
    smoothed = finish_y(1, lines_y, factors_y, held)
    leading = []
    for part, line_x, line_y, field in zip(parts, lines_x, lines_y, smoothed):
        scale = (line_y.scales / line_y.rates * line_x.rates)[0]
        for k in range(members):
            work[k, :, part] = scale * field[k]
        leading.append(work[:, :, part])
    held = local_x(leading, lines_x, 1, beyond)
    outgoing_x(1, lambda copy: copy.start())
    smoothed = finish_x(1, lines_x, held, responses)
    numerator = jnp.zeros((rows, LANES), jnp.float32)
    for part, line, field in zip(parts, lines_x, smoothed):
        new = controls[:, :, part] + line.scales / line.rates * field
        gradient[:, :, part] = new
        numerator = numerator + jnp.sum(new * (new - prev[:, :, part]), axis=0)
    store_gradient = pltpu.make_async_copy(gradient, gradient_h, store_sem.at[1])
    store_gradient.start()

    halves = denominator[:, parts[0]]
    for part in parts[1:]:
        halves = halves + denominator[:, part]
    slots_s[me, 0:1] = jnp.sum(numerator, axis=0, keepdims=True)
    slots_s[me, 1:2] = halves

    def copy_s(source, peer, place):
        return pltpu.make_async_remote_copy(
            src_ref=slots_s.at[source], dst_ref=slots_s.at[source],
            send_sem=send_s.at[peer], recv_sem=recv_s.at[source],
            device_id=place, device_id_type=MESH)

    each_peer(lambda peer, place: copy_s(me, peer, place).start())
    each_peer(lambda peer, place: copy_s(peer, peer, place).wait_recv())
    sums = jnp.sum(jnp.sum(slots_s[...], axis=0), axis=1, keepdims=True)
    direction[...] = (sums[0:1] / sums[1:2])[None] * old[...] - gradient[...]
    store_direction = pltpu.make_async_copy(direction, direction_h, store_sem.at[2])
    store_direction.start()

    each_peer(lambda peer, place: copy_s(me, peer, place).wait_send())
    for turn in range(2):
        outgoing_x(turn, lambda copy: copy.wait_send())
        for off in range(1, n_gy):
            copy_y(turn, gy, lax.rem(gy + off, n_gy)).wait_send()
    for off in range(1, n_gz):
        copy_z(gz, lax.rem(gz + off, n_gz)).wait_send()
    store_increment.wait()
    store_gradient.wait()
    store_direction.wait()


def results_kernel(*refs):
    count = len(refs) // 2
    sems = refs[-1]
    copies = [pltpu.make_async_copy(refs[i], refs[count + i], sems.at[i]) for i in range(count)]
    for copy in copies:
        copy.start()
    for copy in copies:
        copy.wait()


def shards(
    controls,
    anomalies,
    x_rates,
    y_rates,
    obs_cells,
    obs_codes,
    obs_values,
    obs_weights,
    prev_gradient,
    prev_direction,
):
    n_gx, n_gy, n_gz = (lax.axis_size(name) for name in ("gx", "gy", "gz"))
    total = n_gx * n_gy * n_gz
    members, rows, columns = controls.shape
    packed = -(-(members + 1) // rows) * rows
    args = (controls, anomalies, x_rates, y_rates, obs_cells, obs_codes, obs_values, obs_weights, prev_gradient,
            prev_direction)
    dma = pltpu.SemaphoreType.DMA
    anywhere = pl.BlockSpec(memory_space=pl.ANY)
    results = tuple(
        jax.ShapeDtypeStruct(shape, jnp.float32)
        for shape in (controls.shape, controls.shape, (2, rows, columns)))
    held = pl.pallas_call(
        functools.partial(kernel, (n_gx, n_gy, n_gz)),
        out_shape=results,
        in_specs=[anywhere] * len(args),
        out_specs=(anywhere,) * len(results),
        scratch_shapes=[pltpu.VMEM(a.shape, a.dtype) for a in args] + [
            pltpu.VMEM(controls.shape, jnp.float32),
            pltpu.VMEM(controls.shape, jnp.float32),
            pltpu.VMEM((2, rows, columns), jnp.float32),
            pltpu.VMEM(controls.shape, jnp.float32),
            pltpu.VMEM((2, packed, columns), jnp.float32),
            pltpu.VMEM((2, n_gx, 2, packed, columns), jnp.float32),
            pltpu.VMEM((2, n_gy, 2, rows, LANES), jnp.float32),
            pltpu.VMEM((n_gz, 2, rows, columns), jnp.float32),
            pltpu.VMEM((total, 2, LANES), jnp.float32),
            pltpu.VMEM((columns, obs_cells.shape[-1])[::-1], jnp.bfloat16),
            dma((len(args),)), dma((3,)),
            dma((2, 2, n_gx)), dma((2, 2, n_gx)),
            dma((2, n_gy)), dma((2, n_gy)),
            dma((n_gz,)), dma((n_gz,)),
            dma((total,)), dma((total,)),
        ],
        compiler_params=pltpu.CompilerParams(
            collective_id=0, has_side_effects=True, vmem_limit_bytes=VMEM_BYTES
        ),
    )(*args)
    return pl.pallas_call(
        results_kernel,
        out_shape=results,
        in_specs=[anywhere] * len(results),
        out_specs=(anywhere,) * len(results),
        scratch_shapes=[dma((len(results),))],
        compiler_params=pltpu.CompilerParams(vmem_limit_bytes=VMEM_BYTES),
    )(*held)


def solution(mesh):
    in_specs = (
        P("gz", ("grp", "gx"), "gy"),
        P(None, "gz", ("grp", "gx"), "gy"),
        P(("grp", "gx"), "gy"),
        P(("grp", "gx"), "gy"),
        P(("grp", "gx"), "gy", None),
        P(("grp", "gx"), "gy", None),
        P(("grp", "gx"), "gy", None),
        P(("grp", "gx"), "gy", None),
        P("gz", ("grp", "gx"), "gy"),
        P("gz", ("grp", "gx"), "gy"),
    )
    out_specs = (
        P("gz", ("grp", "gx"), "gy"),
        P("gz", ("grp", "gx"), "gy"),
        P(None, ("grp", "gx"), "gy"),
    )
    return jax.shard_map(shards, mesh=mesh, in_specs=in_specs, out_specs=out_specs, check_vma=False)
```

```python
import functools
import math

import jax
import jax.numpy as jnp
from jax import lax
from jax.experimental import pallas as pl
from jax.experimental.pallas import tpu as pltpu
from jax.sharding import PartitionSpec as P

NDIR = 72
LANES = 128
VMEM_BYTES = 63 * 1024 * 1024
MESH = pl.DeviceIdType.MESH


def rolled(values, shift, axis):
    return pltpu.roll(values, shift % values.shape[axis], axis)


def ladder(rates, axis, reverse):
    size = rates.shape[axis]
    place = lax.broadcasted_iota(jnp.int32, rates.shape, axis)
    factor = jnp.where(place == (size - 1 if reverse else 0), 0.0, rates)
    steps = []
    d = 1
    while d < size:
        shift = -d if reverse else d
        steps.append((shift, factor))
        factor = factor * rolled(factor, shift, axis)
        d *= 2
    return steps


def run(steps, values, axis):
    for shift, factor in steps:
        values = values + factor * rolled(values, shift, axis)
    return values


class Line:
    def __init__(self, rates, axis):
        self.axis = axis
        self.rates = rates
        self.scales = jnp.sqrt(1.0 - rates * rates)
        self.forward = ladder(rates, axis, False)
        self.backward = ladder(rates, axis, True)
        place = lax.broadcasted_iota(jnp.int32, rates.shape, axis)
        self.onward = run(self.forward, jnp.where(place == 0, rates, 0.0), axis)
        self.back = run(self.backward, jnp.where(place == rates.shape[axis] - 1, rates, 0.0), axis)
        self.echo = run(self.backward, self.scales * self.onward, axis)

    def local(self, leading):
        inward = run(self.forward, leading, self.axis)
        return inward, run(self.backward, self.scales * inward, self.axis)


def split_three(values):
    high = values.astype(jnp.bfloat16)
    rest = values - high.astype(jnp.float32)
    middle = rest.astype(jnp.bfloat16)
    low = (rest - middle.astype(jnp.float32)).astype(jnp.bfloat16)
    return jnp.concatenate([high, middle, low], axis=0)


def kernel(
    sizes,
    controls_h, anomalies_h, x_rates_h, y_rates_h, cells_h, codes_h, values_h, weights_h, prev_h, old_h,
    gradient_h, direction_h, increment_h,
    controls, anomalies, x_rates, y_rates, cells, codes, values, weights, prev, old,
    gradient, direction, increment, work, enter, slots_x, slots_y, slots_z, slots_a, slots_s, of_column,
    load_sem, store_sem, send_x, recv_x, send_y, recv_y, send_z, recv_z, send_s, recv_s,
):
    n_gx, n_gy, n_gz = sizes
    total = n_gx * n_gy * n_gz
    gx, gy, gz = (lax.axis_index(name) for name in ("gx", "gy", "gz"))
    me = (gx * n_gy + gy) * n_gz + gz
    members, rows, columns = controls.shape
    parts = [slice(at, at + LANES) for at in range(0, columns, LANES)]
    spread = 1.0 / math.sqrt(members * n_gz - 1)

    near = [(lax.rem(gy + b, n_gy), lax.rem(gz + c, n_gz)) for b in range(n_gy) for c in range(n_gz)]

    def each_peer(body):
        def visit(x, others):
            for y, z in others:
                body((x * n_gy + y) * n_gz + z, {"gx": x, "gy": y, "gz": z})

        visit(gx, near[1:])
        if n_gx <= 4:
            for off in range(1, n_gx):
                visit(lax.rem(gx + off, n_gx), near)
        else:
            lax.fori_loop(1, n_gx, lambda off, c: (visit(lax.rem(gx + off, n_gx), near), c)[1], 0)

    barrier = pltpu.get_barrier_semaphore()
    each_peer(lambda index, place: pl.semaphore_signal(
        barrier, inc=1, device_id=place, device_id_type=MESH))

    loads = [
        pltpu.make_async_copy(src, dst, load_sem.at[i])
        for i, (src, dst) in enumerate((
            (x_rates_h, x_rates), (controls_h, controls), (y_rates_h, y_rates),
            (anomalies_h, anomalies), (cells_h, cells), (codes_h, codes), (values_h, values),
            (weights_h, weights), (prev_h, prev), (old_h, old)))
    ]
    for load in loads:
        load.start()

    row_at = lax.broadcasted_iota(jnp.int32, (rows, LANES), 0)
    lane_at = lax.broadcasted_iota(jnp.int32, (rows, LANES), 1)

    def pack_rows(blocks, from_row, group):
        tile = jnp.zeros((rows, LANES), jnp.float32)
        for s, block in enumerate(blocks[group * rows:(group + 1) * rows]):
            tile = jnp.where(row_at == s, rolled(block, s - from_row, 0), tile)
        return tile

    def local_x(leading, lines, turn, beyond=None):
        outs = []
        for at, (part, line, lead) in enumerate(zip(parts, lines, leading)):
            inward, outward = line.local(lead)
            ends = [inward[k] for k in range(members)] + [line.onward[0]]
            heads = [outward[k] for k in range(members)] + [line.echo[0]]
            for group in range(slots_x.shape[3] // rows):
                here = pl.ds(group * rows, rows)
                end = pack_rows(ends, rows - 1, group)
                head = pack_rows(heads, 0, group)
                if beyond is not None:
                    head = head + beyond[at] * end
                slots_x[turn, gx, 0, here, part] = end
                slots_x[turn, gx, 1, here, part] = head
            outs.append(outward)
        return outs

    def copy_x(turn, kind, source, peer):
        return pltpu.make_async_remote_copy(
            src_ref=slots_x.at[turn, source, kind], dst_ref=slots_x.at[turn, source, kind],
            send_sem=send_x.at[turn, kind, peer], recv_sem=recv_x.at[turn, kind, source],
            device_id={"gx": peer}, device_id_type=MESH)

    def outgoing_x(turn, act):
        for off in range(1, n_gx):
            peer = lax.rem(gx + off, n_gx)

            @pl.when(gx < n_gx - 1 if turn == 0 else peer > gx)
            def _():
                act(copy_x(turn, 0, gx, peer))

            @pl.when(peer < gx)
            def _():
                act(copy_x(turn, 1, gx, peer))

    def incoming_x(turn):
        for off in range(1, n_gx):
            source = lax.rem(gx + off, n_gx)

            @pl.when(source < n_gx - 1 if turn == 0 else source < gx)
            def _():
                copy_x(turn, 0, source, source).wait_recv()

            @pl.when(source > gx)
            def _():
                copy_x(turn, 1, source, source).wait_recv()

    def states_x(turn, part):
        state = jnp.zeros((slots_x.shape[3], LANES), jnp.float32)
        states = [state]
        mine = state
        for t in range(n_gx - 1):
            through = slots_x[0, t, 0, members:members + 1, part]
            state = through * state + slots_x[turn, t, 0, :, part]
            states.append(state)
            mine = jnp.where(gx == t + 1, state, mine)
        return states, mine

    def backward_x(turn, part, states):
        state = jnp.zeros((slots_x.shape[3], LANES), jnp.float32)
        mine = state
        for t in range(n_gx - 1, 0, -1):
            if t < n_gx - 1:
                state = slots_x[0, t, 0, members:members + 1, part] * state
            state = state + slots_x[turn, t, 1, :, part]
            if states is not None:
                state = state + slots_x[0, t, 1, members:members + 1, part] * states[t]
            mine = jnp.where(gx == t - 1, state, mine)
        return mine

    def response_x(part):
        factor = jnp.zeros((1, LANES), jnp.float32)
        mine = factor
        for t in range(n_gx - 1, 0, -1):
            if t < n_gx - 1:
                through = slots_x[0, t, 0, members:members + 1, part]
                factor = through * through * factor
            factor = factor + slots_x[0, t, 1, members:members + 1, part]
            mine = jnp.where(gx == t - 1, factor, mine)
        return mine

    def finish_x(turn, lines, outs, responses=None):
        incoming_x(turn)
        results = []
        for at, (part, line, outward) in enumerate(zip(parts, lines, outs)):
            states, mine = states_x(turn, part)
            enter[0, :, part] = mine
            if responses is None:
                enter[1, :, part] = backward_x(turn, part, states)
            else:
                leaving = slots_x[0, gx, 0, members:members + 1, part] * mine + slots_x[turn, gx, 0, :, part]
                enter[1, :, part] = backward_x(turn, part, None) + responses[at] * leaving
            for k in range(members):
                first = jnp.broadcast_to(enter[0, k:k + 1, part], (rows, LANES))
                second = jnp.broadcast_to(enter[1, k:k + 1, part], (rows, LANES))
                work[k, :, part] = outward[k] + line.echo[0] * first + line.back[0] * second
            results.append(work[:, :, part])
        return results

    def pack_lanes(field, from_lane):
        tile = jnp.zeros((rows, LANES), jnp.float32)
        for k in range(members):
            tile = jnp.where(lane_at == k, rolled(field[k], k - from_lane, 1), tile)
        return tile

    def across(tile, lane):
        return jnp.broadcast_to(tile[:, lane:lane + 1], (rows, LANES))

    def local_y(leading, lines, turn):
        outs = []
        for s, (line, lead) in enumerate(zip(lines, leading)):
            inward, outward = line.local(lead)
            slots_y[turn, gy, gz, s, 0] = jnp.where(
                lane_at == members, across(line.onward[0], LANES - 1), pack_lanes(inward, LANES - 1))
            slots_y[turn, gy, gz, s, 1] = jnp.where(
                lane_at == members, across(line.echo[0], 0), pack_lanes(outward, 0))
            outs.append(outward)
        return outs

    def each_y(turn, act):
        for y, z in near[1:] if turn == 0 else [near[b * n_gz] for b in range(1, n_gy)]:
            act(y, z)

    def copy_y(turn, source, peer):
        slot = (turn, *source)
        return pltpu.make_async_remote_copy(
            src_ref=slots_y.at[slot], dst_ref=slots_y.at[slot],
            send_sem=send_y.at[turn, *peer], recv_sem=recv_y.at[turn, *source],
            device_id={"gy": peer[0], "gz": peer[1]}, device_id_type=MESH)

    def start_y(turn):
        each_y(turn, lambda *peer: copy_y(turn, (gy, gz), peer).start())

    def entering_y(turn, z):
        chain = [(t, s) for t in range(n_gy) for s in range(len(parts))]
        state = jnp.zeros((rows, LANES), jnp.float32)
        states = []
        firsts = [state] * len(parts)
        for t, s in chain:
            states.append(state)
            firsts[s] = state if t == 0 else jnp.where(gy == t, state, firsts[s])
            tile = slots_y[turn, t, z, s, 0]
            state = across(tile, members) * state + tile
        state = jnp.zeros((rows, LANES), jnp.float32)
        seconds = [state] * len(parts)
        for (t, s), entered in reversed(list(zip(chain, states))):
            seconds[s] = state if t == n_gy - 1 else jnp.where(gy == t, state, seconds[s])
            tile = slots_y[turn, t, z, s, 1]
            state = across(slots_y[turn, t, z, s, 0], members) * state + tile + across(tile, members) * entered
        return firsts, seconds

    def copy_z(source, peer):
        return pltpu.make_async_remote_copy(
            src_ref=slots_z.at[source], dst_ref=slots_z.at[source],
            send_sem=send_z.at[0, peer], recv_sem=recv_z.at[0, source],
            device_id={"gz": peer}, device_id_type=MESH)

    def copy_a(source, peer):
        return pltpu.make_async_remote_copy(
            src_ref=slots_a.at[source], dst_ref=slots_a.at[source],
            send_sem=send_z.at[1, peer], recv_sem=recv_z.at[1, source],
            device_id={"gz": peer}, device_id_type=MESH)

    other_z = [lax.rem(gz + off, n_gz) for off in range(1, n_gz)]

    loads[0].wait()
    lines_x = [Line(x_rates[:, part][None], 1) for part in parts]
    loads[1].wait()
    held = local_x([line.scales * controls[:, :, part] for part, line in zip(parts, lines_x)], lines_x, 0)
    pl.semaphore_wait(barrier, total - 1)
    outgoing_x(0, lambda copy: copy.start())

    loads[2].wait()
    lines_y = [Line(y_rates[:, part][None], 2) for part in parts]
    for load in loads[3:]:
        load.wait()
    slots_a[gz] = anomalies[...].astype(jnp.float32)
    for z in other_z:
        copy_a(gz, z).start()
    n_obs = cells.shape[-1]
    cell = cells[0]
    bits = columns.bit_length() - 1
    cell_row = lax.shift_right_logical(cell, jnp.full_like(cell, bits))
    cell_column = cell & (columns - 1)
    bearing = codes[0].astype(jnp.float32) * (2.0 * math.pi / NDIR)
    cosine = jnp.cos(bearing)
    sine = jnp.sin(bearing)
    hit = (lax.broadcasted_iota(jnp.int32, (columns, n_obs), 0) == cell_column).astype(jnp.float32)
    at_column = hit.astype(jnp.bfloat16)
    of_column[...] = hit.T.astype(jnp.bfloat16)
    in_row = lax.broadcasted_iota(jnp.int32, (rows, n_obs), 0) == cell_row
    toward = jnp.concatenate([jnp.where(in_row, cosine, 0.0), jnp.where(in_row, sine, 0.0)], axis=0)
    before = prev[...]
    denominator = jnp.sum(jnp.sum(before * before, axis=0), axis=0, keepdims=True)

    filtered = finish_x(0, lines_x, held)

    outs = local_y([line.scales * v for line, v in zip(lines_y, filtered)], lines_y, 0)
    start_y(0)
    for c in range(2):
        for part, field in zip(parts, outs):
            slots_z[gz, c, :, part] = jnp.sum(slots_a[gz, c, :, :, part] * field, axis=0)
    for z in other_z:
        copy_z(gz, z).start()
    responses = [response_x(part) for part in parts]
    beyond = [line.onward[0, rows - 1:] * response for line, response in zip(lines_x, responses)]
    for z in other_z:
        copy_a(z, z).wait_recv()
    each_y(0, lambda *source: copy_y(0, source, source).wait_recv())
    for z in other_z:
        copy_z(z, z).wait_recv()
    for z in range(n_gz):
        firsts, seconds = entering_y(0, z)
        for s, (part, line) in enumerate(zip(parts, lines_y)):
            sums = [[jnp.zeros((rows, LANES), jnp.float32)] * 2 for _ in range(2)]
            for k in range(members):
                for e, state in enumerate((across(firsts[s], k), across(seconds[s], k))):
                    for c in range(2):
                        sums[c][e] = sums[c][e] + slots_a[z, c, k, :, part] * state
            for c in range(2):
                share = slots_z[z, c, :, part] + line.echo[0] * sums[c][0] + line.back[0] * sums[c][1]
                increment[c, :, part] = share if z == 0 else increment[c, :, part] + share
    grown = increment[...] * spread
    increment[...] = grown
    store_increment = pltpu.make_async_copy(increment, increment_h, store_sem.at[0])
    store_increment.start()

    lifted = jnp.dot(
        split_three(jnp.concatenate([grown[0], grown[1]], axis=0)), at_column,
        preferred_element_type=jnp.float32)
    lifted = lifted[:2 * rows] + (lifted[2 * rows:4 * rows] + lifted[4 * rows:])
    projected = jnp.sum(lifted * toward, axis=0, keepdims=True)
    misfit = weights[0] * (projected - values[0])
    back = jnp.dot(
        split_three(toward * misfit), of_column[...], preferred_element_type=jnp.float32)
    back = (back[:2 * rows] + (back[2 * rows:4 * rows] + back[4 * rows:])) * spread

    leading = []
    for part, line in zip(parts, lines_y):
        pulled = (slots_a[gz, 0, :, :, part] * back[None, :rows, part]
                  + slots_a[gz, 1, :, :, part] * back[None, rows:, part])
        leading.append(line.rates * pulled)
    outs = local_y(leading, lines_y, 1)
    start_y(1)
    each_y(1, lambda *source: copy_y(1, source, source).wait_recv())
    firsts, seconds = entering_y(1, gz)
    leading = []
    for s, (part, line_x, line_y) in enumerate(zip(parts, lines_x, lines_y)):
        scale = (line_y.scales / line_y.rates * line_x.rates)[0]
        echo, after = scale * line_y.echo[0], scale * line_y.back[0]
        for k in range(members):
            work[k, :, part] = scale * outs[s][k] + echo * across(firsts[s], k) + after * across(seconds[s], k)
        leading.append(work[:, :, part])
    held = local_x(leading, lines_x, 1, beyond)
    outgoing_x(1, lambda copy: copy.start())
    smoothed = finish_x(1, lines_x, held, responses)
    numerator = jnp.zeros((rows, LANES), jnp.float32)
    for part, line, field in zip(parts, lines_x, smoothed):
        new = controls[:, :, part] + line.scales / line.rates * field
        gradient[:, :, part] = new
        numerator = numerator + jnp.sum(new * (new - prev[:, :, part]), axis=0)
    store_gradient = pltpu.make_async_copy(gradient, gradient_h, store_sem.at[1])
    store_gradient.start()

    halves = denominator[:, parts[0]]
    for part in parts[1:]:
        halves = halves + denominator[:, part]
    slots_s[me, 0:1] = jnp.sum(numerator, axis=0, keepdims=True)
    slots_s[me, 1:2] = halves

    def copy_s(source, peer, place):
        return pltpu.make_async_remote_copy(
            src_ref=slots_s.at[source], dst_ref=slots_s.at[source],
            send_sem=send_s.at[peer], recv_sem=recv_s.at[source],
            device_id=place, device_id_type=MESH)

    each_peer(lambda peer, place: copy_s(me, peer, place).start())
    each_peer(lambda peer, place: copy_s(peer, peer, place).wait_recv())
    sums = jnp.sum(jnp.sum(slots_s[...], axis=0), axis=1, keepdims=True)
    direction[...] = (sums[0:1] / sums[1:2])[None] * old[...] - gradient[...]
    store_direction = pltpu.make_async_copy(direction, direction_h, store_sem.at[2])
    store_direction.start()

    each_peer(lambda peer, place: copy_s(me, peer, place).wait_send())
    for turn in range(2):
        outgoing_x(turn, lambda copy: copy.wait_send())
        each_y(turn, lambda *peer: copy_y(turn, (gy, gz), peer).wait_send())
    for z in other_z:
        copy_z(gz, z).wait_send()
        copy_a(gz, z).wait_send()
    store_increment.wait()
    store_gradient.wait()
    store_direction.wait()


def results_kernel(*refs):
    count = len(refs) // 3
    sems = refs[-1]
    loads = [pltpu.make_async_copy(refs[i], refs[2 * count + i], sems.at[0, i]) for i in range(count)]
    stores = [pltpu.make_async_copy(refs[2 * count + i], refs[count + i], sems.at[1, i]) for i in range(count)]
    for load in loads:
        load.start()
    for load, store in zip(loads, stores):
        load.wait()
        store.start()
    for store in stores:
        store.wait()


def shards(
    controls,
    anomalies,
    x_rates,
    y_rates,
    obs_cells,
    obs_codes,
    obs_values,
    obs_weights,
    prev_gradient,
    prev_direction,
):
    n_gx, n_gy, n_gz = (lax.axis_size(name) for name in ("gx", "gy", "gz"))
    total = n_gx * n_gy * n_gz
    members, rows, columns = controls.shape
    packed = -(-(members + 1) // rows) * rows
    args = (controls, anomalies, x_rates, y_rates, obs_cells, obs_codes, obs_values, obs_weights, prev_gradient,
            prev_direction)
    dma = pltpu.SemaphoreType.DMA
    anywhere = pl.BlockSpec(memory_space=pl.ANY)
    results = tuple(
        jax.ShapeDtypeStruct(shape, jnp.float32)
        for shape in (controls.shape, controls.shape, (2, rows, columns)))
    held = pl.pallas_call(
        functools.partial(kernel, (n_gx, n_gy, n_gz)),
        out_shape=results,
        in_specs=[anywhere] * len(args),
        out_specs=(anywhere,) * len(results),
        scratch_shapes=[pltpu.VMEM(a.shape, a.dtype) for a in args] + [
            pltpu.VMEM(controls.shape, jnp.float32),
            pltpu.VMEM(controls.shape, jnp.float32),
            pltpu.VMEM((2, rows, columns), jnp.float32),
            pltpu.VMEM(controls.shape, jnp.float32),
            pltpu.VMEM((2, packed, columns), jnp.float32),
            pltpu.VMEM((2, n_gx, 2, packed, columns), jnp.float32),
            pltpu.VMEM((2, n_gy, n_gz, columns // LANES, 2, rows, LANES), jnp.float32),
            pltpu.VMEM((n_gz, 2, rows, columns), jnp.float32),
            pltpu.VMEM((n_gz, *anomalies.shape), jnp.float32),
            pltpu.VMEM((total, 2, LANES), jnp.float32),
            pltpu.VMEM((columns, obs_cells.shape[-1])[::-1], jnp.bfloat16),
            dma((len(args),)), dma((3,)),
            dma((2, 2, n_gx)), dma((2, 2, n_gx)),
            dma((2, n_gy, n_gz)), dma((2, n_gy, n_gz)),
            dma((2, n_gz)), dma((2, n_gz)),
            dma((total,)), dma((total,)),
        ],
        compiler_params=pltpu.CompilerParams(
            collective_id=0, has_side_effects=True, vmem_limit_bytes=VMEM_BYTES
        ),
    )(*args)
    return pl.pallas_call(
        results_kernel,
        out_shape=results,
        in_specs=[anywhere] * len(results),
        out_specs=(anywhere,) * len(results),
        scratch_shapes=[pltpu.VMEM(a.shape, a.dtype) for a in results] + [dma((2, len(results)))],
        compiler_params=pltpu.CompilerParams(vmem_limit_bytes=VMEM_BYTES),
    )(*held)


def solution(mesh):
    in_specs = (
        P("gz", ("grp", "gx"), "gy"),
        P(None, "gz", ("grp", "gx"), "gy"),
        P(("grp", "gx"), "gy"),
        P(("grp", "gx"), "gy"),
        P(("grp", "gx"), "gy", None),
        P(("grp", "gx"), "gy", None),
        P(("grp", "gx"), "gy", None),
        P(("grp", "gx"), "gy", None),
        P("gz", ("grp", "gx"), "gy"),
        P("gz", ("grp", "gx"), "gy"),
    )
    out_specs = (
        P("gz", ("grp", "gx"), "gy"),
        P("gz", ("grp", "gx"), "gy"),
        P(None, ("grp", "gx"), "gy"),
    )
    return jax.shard_map(shards, mesh=mesh, in_specs=in_specs, out_specs=out_specs, check_vma=False)
```

```python
import functools
import math

import jax
import jax.numpy as jnp
from jax import lax
from jax.experimental import pallas as pl
from jax.experimental.pallas import tpu as pltpu
from jax.sharding import PartitionSpec as P

NDIR = 72
LANES = 128
VMEM_BYTES = 63 * 1024 * 1024
MESH = pl.DeviceIdType.MESH


def rolled(values, shift, axis):
    return pltpu.roll(values, shift % values.shape[axis], axis)


def step_count(size):
    return (size - 1).bit_length()


class Line:
    def __init__(self, rates, onward, back, echo):
        self.rates = rates
        self.scales = jnp.sqrt(1.0 - rates * rates)
        self.onward, self.back, self.echo = onward, back, echo


class Filter:
    def __init__(self, rates, axis, ladder):
        self.axis, self.ladder = axis, ladder
        self.size = rates[0].shape[axis]
        self.steps = step_count(self.size)
        place = lax.broadcasted_iota(jnp.int32, rates[0].shape, axis)
        first, last = place == 0, place == self.size - 1

        def grow(step, factors):
            grown = []
            for at, factor in enumerate(factors):
                way, group = divmod(at, len(rates))
                ladder[way, group, step] = factor
                grown.append(factor * pltpu.roll(factor, self.shift(step, way), axis))
            return tuple(grown)

        edges = [jnp.where(first, 0.0, r) for r in rates] + [jnp.where(last, 0.0, r) for r in rates]
        lax.fori_loop(0, self.steps, grow, tuple(edges))
        onward = self.run(0, [jnp.where(first, r, 0.0)[None] for r in rates])
        back = self.run(1, [jnp.where(last, r, 0.0)[None] for r in rates])
        scales = [jnp.sqrt(1.0 - r * r) for r in rates]
        echo = self.run(1, [s * o for s, o in zip(scales, onward)])
        self.lines = [Line(*each) for each in zip(rates, *([v[0] for v in vs] for vs in (onward, back, echo)))]

    def shift(self, step, way):
        reach = lax.shift_left(jnp.int32(1), jnp.int32(step))
        return self.size - reach if way else reach

    def run(self, way, values):
        def advance(step, held):
            shift = self.shift(step, way)
            return tuple(
                v + self.ladder[way, group, step][None] * pltpu.roll(v, shift, self.axis + 1)
                for group, v in enumerate(held))

        return lax.fori_loop(0, self.steps, advance, tuple(values))

    def local(self, leading):
        inward = self.run(0, leading)
        return inward, self.run(1, [line.scales * v for line, v in zip(self.lines, inward)])


def split_three(values):
    high = values.astype(jnp.bfloat16)
    rest = values - high.astype(jnp.float32)
    middle = rest.astype(jnp.bfloat16)
    low = (rest - middle.astype(jnp.float32)).astype(jnp.bfloat16)
    return jnp.concatenate([high, middle, low], axis=0)


def kernel(
    sizes,
    controls_h, anomalies_h, x_rates_h, y_rates_h, cells_h, codes_h, values_h, weights_h, prev_h,
    gradient_h, ratio_h, increment_h,
    controls, anomalies, x_rates, y_rates, cells, codes, values, weights, prev,
    gradient, ratio, increment, work, enter, slots_x, slots_y, slots_z, slots_a, slots_s, of_column, ladder_x, ladder_y,
    load_sem, store_sem, send_x, recv_x, send_y, recv_y, send_z, recv_z, send_s, recv_s,
):
    n_gx, n_gy, n_gz = sizes
    total = n_gx * n_gy * n_gz
    gx, gy, gz = (lax.axis_index(name) for name in ("gx", "gy", "gz"))
    me = (gx * n_gy + gy) * n_gz + gz
    members, rows, columns = controls.shape
    parts = [slice(at, at + LANES) for at in range(0, columns, LANES)]
    spread = 1.0 / math.sqrt(members * n_gz - 1)

    near = [(lax.rem(gy + b, n_gy), lax.rem(gz + c, n_gz)) for b in range(n_gy) for c in range(n_gz)]

    def each_peer(body):
        def visit(x, others):
            for y, z in others:
                body((x * n_gy + y) * n_gz + z, {"gx": x, "gy": y, "gz": z})

        visit(gx, near[1:])
        if n_gx <= 4:
            for off in range(1, n_gx):
                visit(lax.rem(gx + off, n_gx), near)
        else:
            lax.fori_loop(1, n_gx, lambda off, c: (visit(lax.rem(gx + off, n_gx), near), c)[1], 0)

    barrier = pltpu.get_barrier_semaphore()
    each_peer(lambda index, place: pl.semaphore_signal(
        barrier, inc=1, device_id=place, device_id_type=MESH))

    loads = [
        pltpu.make_async_copy(src, dst, load_sem.at[i])
        for i, (src, dst) in enumerate((
            (x_rates_h, x_rates), (controls_h, controls), (y_rates_h, y_rates),
            (anomalies_h, anomalies), (cells_h, cells), (codes_h, codes), (values_h, values),
            (weights_h, weights), (prev_h, prev)))
    ]
    for load in loads:
        load.start()

    row_at = lax.broadcasted_iota(jnp.int32, (rows, LANES), 0)
    lane_at = lax.broadcasted_iota(jnp.int32, (rows, LANES), 1)

    def pack_rows(blocks, from_row, group):
        tile = jnp.zeros((rows, LANES), jnp.float32)
        for s, block in enumerate(blocks[group * rows:(group + 1) * rows]):
            tile = jnp.where(row_at == s, rolled(block, s - from_row, 0), tile)
        return tile

    def local_x(leading, turn, beyond=None):
        outs = []
        fields = along_x.local(leading)
        for at, (part, line, inward, outward) in enumerate(zip(parts, along_x.lines, *fields)):
            ends = [inward[k] for k in range(members)] + [line.onward]
            heads = [outward[k] for k in range(members)] + [line.echo]
            for group in range(slots_x.shape[3] // rows):
                here = pl.ds(group * rows, rows)
                end = pack_rows(ends, rows - 1, group)
                head = pack_rows(heads, 0, group)
                if beyond is not None:
                    head = head + beyond[at] * end
                slots_x[turn, gx, 0, here, part] = end
                slots_x[turn, gx, 1, here, part] = head
            outs.append(outward)
        return outs

    def copy_x(turn, kind, source, peer):
        return pltpu.make_async_remote_copy(
            src_ref=slots_x.at[turn, source, kind], dst_ref=slots_x.at[turn, source, kind],
            send_sem=send_x.at[turn, kind, peer], recv_sem=recv_x.at[turn, kind, source],
            device_id={"gx": peer}, device_id_type=MESH)

    def outgoing_x(turn, act):
        for off in range(1, n_gx):
            peer = lax.rem(gx + off, n_gx)

            @pl.when(gx < n_gx - 1 if turn == 0 else peer > gx)
            def _():
                act(copy_x(turn, 0, gx, peer))

            @pl.when(peer < gx)
            def _():
                act(copy_x(turn, 1, gx, peer))

    def incoming_x(turn):
        for off in range(1, n_gx):
            source = lax.rem(gx + off, n_gx)

            @pl.when(source < n_gx - 1 if turn == 0 else source < gx)
            def _():
                copy_x(turn, 0, source, source).wait_recv()

            @pl.when(source > gx)
            def _():
                copy_x(turn, 1, source, source).wait_recv()

    def states_x(turn, part):
        state = jnp.zeros((slots_x.shape[3], LANES), jnp.float32)
        states = [state]
        mine = state
        for t in range(n_gx - 1):
            through = slots_x[0, t, 0, members:members + 1, part]
            state = through * state + slots_x[turn, t, 0, :, part]
            states.append(state)
            mine = jnp.where(gx == t + 1, state, mine)
        return states, mine

    def backward_x(turn, part, states):
        state = jnp.zeros((slots_x.shape[3], LANES), jnp.float32)
        mine = state
        for t in range(n_gx - 1, 0, -1):
            if t < n_gx - 1:
                state = slots_x[0, t, 0, members:members + 1, part] * state
            state = state + slots_x[turn, t, 1, :, part]
            if states is not None:
                state = state + slots_x[0, t, 1, members:members + 1, part] * states[t]
            mine = jnp.where(gx == t - 1, state, mine)
        return mine

    def response_x(part):
        factor = jnp.zeros((1, LANES), jnp.float32)
        mine = factor
        for t in range(n_gx - 1, 0, -1):
            if t < n_gx - 1:
                through = slots_x[0, t, 0, members:members + 1, part]
                factor = through * through * factor
            factor = factor + slots_x[0, t, 1, members:members + 1, part]
            mine = jnp.where(gx == t - 1, factor, mine)
        return mine

    def finish_x(turn, lines, outs, responses=None):
        incoming_x(turn)
        results = []
        for at, (part, line, outward) in enumerate(zip(parts, lines, outs)):
            states, mine = states_x(turn, part)
            enter[0, :, part] = mine
            if responses is None:
                enter[1, :, part] = backward_x(turn, part, states)
            else:
                leaving = slots_x[0, gx, 0, members:members + 1, part] * mine + slots_x[turn, gx, 0, :, part]
                enter[1, :, part] = backward_x(turn, part, None) + responses[at] * leaving
            for k in range(members):
                first = jnp.broadcast_to(enter[0, k:k + 1, part], (rows, LANES))
                second = jnp.broadcast_to(enter[1, k:k + 1, part], (rows, LANES))
                work[k, :, part] = outward[k] + line.echo * first + line.back * second
            results.append(work[:, :, part])
        return results

    def pack_lanes(field, from_lane):
        tile = jnp.zeros((rows, LANES), jnp.float32)
        for k in range(members):
            tile = jnp.where(lane_at == k, rolled(field[k], k - from_lane, 1), tile)
        return tile

    def across(tile, lane):
        return jnp.broadcast_to(tile[:, lane:lane + 1], (rows, LANES))

    def local_y(leading, turn):
        outs = []
        fields = along_y.local(leading)
        for s, (line, inward, outward) in enumerate(zip(along_y.lines, *fields)):
            slots_y[turn, gy, gz, s, 0] = jnp.where(
                lane_at == members, across(line.onward, LANES - 1), pack_lanes(inward, LANES - 1))
            slots_y[turn, gy, gz, s, 1] = jnp.where(
                lane_at == members, across(line.echo, 0), pack_lanes(outward, 0))
            outs.append(outward)
        return outs

    def each_y(turn, act):
        for y, z in near[1:] if turn == 0 else [near[b * n_gz] for b in range(1, n_gy)]:
            act(y, z)

    def copy_y(turn, source, peer):
        slot = (turn, *source)
        return pltpu.make_async_remote_copy(
            src_ref=slots_y.at[slot], dst_ref=slots_y.at[slot],
            send_sem=send_y.at[turn, *peer], recv_sem=recv_y.at[turn, *source],
            device_id={"gy": peer[0], "gz": peer[1]}, device_id_type=MESH)

    def start_y(turn):
        each_y(turn, lambda *peer: copy_y(turn, (gy, gz), peer).start())

    def entering_y(turn, z):
        chain = [(t, s) for t in range(n_gy) for s in range(len(parts))]
        state = jnp.zeros((rows, LANES), jnp.float32)
        states = []
        firsts = [state] * len(parts)
        for t, s in chain:
            states.append(state)
            firsts[s] = state if t == 0 else jnp.where(gy == t, state, firsts[s])
            tile = slots_y[turn, t, z, s, 0]
            state = across(tile, members) * state + tile
        state = jnp.zeros((rows, LANES), jnp.float32)
        seconds = [state] * len(parts)
        for (t, s), entered in reversed(list(zip(chain, states))):
            seconds[s] = state if t == n_gy - 1 else jnp.where(gy == t, state, seconds[s])
            tile = slots_y[turn, t, z, s, 1]
            state = across(slots_y[turn, t, z, s, 0], members) * state + tile + across(tile, members) * entered
        return firsts, seconds

    def copy_z(source, peer):
        return pltpu.make_async_remote_copy(
            src_ref=slots_z.at[source], dst_ref=slots_z.at[source],
            send_sem=send_z.at[0, peer], recv_sem=recv_z.at[0, source],
            device_id={"gz": peer}, device_id_type=MESH)

    def copy_a(source, peer):
        return pltpu.make_async_remote_copy(
            src_ref=slots_a.at[source], dst_ref=slots_a.at[source],
            send_sem=send_z.at[1, peer], recv_sem=recv_z.at[1, source],
            device_id={"gz": peer}, device_id_type=MESH)

    other_z = [lax.rem(gz + off, n_gz) for off in range(1, n_gz)]

    loads[0].wait()
    along_x = Filter([x_rates[:, part] for part in parts], 0, ladder_x)
    lines_x = along_x.lines
    loads[1].wait()
    held = local_x([line.scales * controls[:, :, part] for part, line in zip(parts, lines_x)], 0)
    pl.semaphore_wait(barrier, total - 1)
    outgoing_x(0, lambda copy: copy.start())

    loads[2].wait()
    along_y = Filter([y_rates[:, part] for part in parts], 1, ladder_y)
    lines_y = along_y.lines
    for load in loads[3:]:
        load.wait()
    slots_a[gz] = anomalies[...].astype(jnp.float32)
    for z in other_z:
        copy_a(gz, z).start()
    n_obs = cells.shape[-1]
    cell = cells[0]
    bits = columns.bit_length() - 1
    cell_row = lax.shift_right_logical(cell, jnp.full_like(cell, bits))
    cell_column = cell & (columns - 1)
    bearing = codes[0].astype(jnp.float32) * (2.0 * math.pi / NDIR)
    cosine = jnp.cos(bearing)
    sine = jnp.sin(bearing)
    hit = (lax.broadcasted_iota(jnp.int32, (columns, n_obs), 0) == cell_column).astype(jnp.float32)
    at_column = hit.astype(jnp.bfloat16)
    of_column[...] = hit.T.astype(jnp.bfloat16)
    in_row = lax.broadcasted_iota(jnp.int32, (rows, n_obs), 0) == cell_row
    toward = jnp.concatenate([jnp.where(in_row, cosine, 0.0), jnp.where(in_row, sine, 0.0)], axis=0)
    before = prev[...]
    denominator = jnp.sum(jnp.sum(before * before, axis=0), axis=0, keepdims=True)

    filtered = finish_x(0, lines_x, held)

    outs = local_y([line.scales * v for line, v in zip(lines_y, filtered)], 0)
    start_y(0)
    for c in range(2):
        for part, field in zip(parts, outs):
            slots_z[gz, c, :, part] = jnp.sum(slots_a[gz, c, :, :, part] * field, axis=0)
    for z in other_z:
        copy_z(gz, z).start()
    responses = [response_x(part) for part in parts]
    beyond = [line.onward[rows - 1:] * response for line, response in zip(lines_x, responses)]
    for z in other_z:
        copy_a(z, z).wait_recv()
    each_y(0, lambda *source: copy_y(0, source, source).wait_recv())
    for z in other_z:
        copy_z(z, z).wait_recv()
    for z in range(n_gz):
        firsts, seconds = entering_y(0, z)
        for s, (part, line) in enumerate(zip(parts, lines_y)):
            sums = [[jnp.zeros((rows, LANES), jnp.float32)] * 2 for _ in range(2)]
            for k in range(members):
                for e, state in enumerate((across(firsts[s], k), across(seconds[s], k))):
                    for c in range(2):
                        sums[c][e] = sums[c][e] + slots_a[z, c, k, :, part] * state
            for c in range(2):
                share = slots_z[z, c, :, part] + line.echo * sums[c][0] + line.back * sums[c][1]
                increment[c, :, part] = share if z == 0 else increment[c, :, part] + share
    grown = increment[...] * spread
    increment[...] = grown
    store_increment = pltpu.make_async_copy(increment, increment_h, store_sem.at[0])
    store_increment.start()

    lifted = jnp.dot(
        split_three(jnp.concatenate([grown[0], grown[1]], axis=0)), at_column,
        preferred_element_type=jnp.float32)
    lifted = lifted[:2 * rows] + (lifted[2 * rows:4 * rows] + lifted[4 * rows:])
    projected = jnp.sum(lifted * toward, axis=0, keepdims=True)
    misfit = weights[0] * (projected - values[0])
    back = jnp.dot(
        split_three(toward * misfit), of_column[...], preferred_element_type=jnp.float32)
    back = (back[:2 * rows] + (back[2 * rows:4 * rows] + back[4 * rows:])) * spread

    leading = []
    for part, line in zip(parts, lines_y):
        pulled = (slots_a[gz, 0, :, :, part] * back[None, :rows, part]
                  + slots_a[gz, 1, :, :, part] * back[None, rows:, part])
        leading.append(line.rates * pulled)
    outs = local_y(leading, 1)
    start_y(1)
    each_y(1, lambda *source: copy_y(1, source, source).wait_recv())
    firsts, seconds = entering_y(1, gz)
    leading = []
    for s, (part, line_x, line_y) in enumerate(zip(parts, lines_x, lines_y)):
        scale = line_y.scales / line_y.rates * line_x.rates
        echo, after = scale * line_y.echo, scale * line_y.back
        for k in range(members):
            work[k, :, part] = scale * outs[s][k] + echo * across(firsts[s], k) + after * across(seconds[s], k)
        leading.append(work[:, :, part])
    held = local_x(leading, 1, beyond)
    outgoing_x(1, lambda copy: copy.start())
    smoothed = finish_x(1, lines_x, held, responses)
    numerator = jnp.zeros((rows, LANES), jnp.float32)
    for part, line, field in zip(parts, lines_x, smoothed):
        new = controls[:, :, part] + line.scales / line.rates * field
        gradient[:, :, part] = new
        numerator = numerator + jnp.sum(new * (new - prev[:, :, part]), axis=0)
    store_gradient = pltpu.make_async_copy(gradient, gradient_h, store_sem.at[1])
    store_gradient.start()

    halves = denominator[:, parts[0]]
    for part in parts[1:]:
        halves = halves + denominator[:, part]
    slots_s[me, 0:1] = jnp.sum(numerator, axis=0, keepdims=True)
    slots_s[me, 1:2] = halves

    def copy_s(source, peer, place):
        return pltpu.make_async_remote_copy(
            src_ref=slots_s.at[source], dst_ref=slots_s.at[source],
            send_sem=send_s.at[peer], recv_sem=recv_s.at[source],
            device_id=place, device_id_type=MESH)

    each_peer(lambda peer, place: copy_s(me, peer, place).start())
    each_peer(lambda peer, place: copy_s(peer, peer, place).wait_recv())
    sums = jnp.sum(jnp.sum(slots_s[...], axis=0), axis=1, keepdims=True)
    ratio[...] = jnp.broadcast_to(sums[0:1] / sums[1:2], ratio.shape)
    store_ratio = pltpu.make_async_copy(ratio, ratio_h, store_sem.at[2])
    store_ratio.start()

    each_peer(lambda peer, place: copy_s(me, peer, place).wait_send())
    for turn in range(2):
        outgoing_x(turn, lambda copy: copy.wait_send())
        each_y(turn, lambda *peer: copy_y(turn, (gy, gz), peer).wait_send())
    for z in other_z:
        copy_z(gz, z).wait_send()
        copy_a(gz, z).wait_send()
    store_increment.wait()
    store_gradient.wait()
    store_ratio.wait()


def results_kernel(
    gradient_h, ratio_h, increment_h, old_h, gradient_out, direction_out, increment_out,
    gradient, ratio, increment, old, direction, load_sem, store_sem,
):
    loads = [
        pltpu.make_async_copy(src, dst, load_sem.at[i])
        for i, (src, dst) in enumerate((
            (ratio_h, ratio), (gradient_h, gradient), (old_h, old), (increment_h, increment)))
    ]
    stores = [
        pltpu.make_async_copy(src, dst, store_sem.at[i])
        for i, (src, dst) in enumerate((
            (gradient, gradient_out), (direction, direction_out), (increment, increment_out)))
    ]
    for load in loads:
        load.start()
    loads[0].wait()
    loads[1].wait()
    stores[0].start()
    loads[2].wait()
    for at in range(0, gradient.shape[2], LANES):
        part = slice(at, at + LANES)
        direction[:, :, part] = ratio[...][None] * old[:, :, part] - gradient[:, :, part]
    stores[1].start()
    loads[3].wait()
    stores[2].start()
    for store in stores:
        store.wait()


def shards(
    controls,
    anomalies,
    x_rates,
    y_rates,
    obs_cells,
    obs_codes,
    obs_values,
    obs_weights,
    prev_gradient,
    prev_direction,
):
    n_gx, n_gy, n_gz = (lax.axis_size(name) for name in ("gx", "gy", "gz"))
    total = n_gx * n_gy * n_gz
    members, rows, columns = controls.shape
    packed = -(-(members + 1) // rows) * rows
    args = (controls, anomalies, x_rates, y_rates, obs_cells, obs_codes, obs_values, obs_weights, prev_gradient)
    dma = pltpu.SemaphoreType.DMA
    anywhere = pl.BlockSpec(memory_space=pl.ANY)
    results = tuple(
        jax.ShapeDtypeStruct(shape, jnp.float32)
        for shape in (controls.shape, (rows, LANES), (2, rows, columns)))
    held = pl.pallas_call(
        functools.partial(kernel, (n_gx, n_gy, n_gz)),
        out_shape=results,
        in_specs=[anywhere] * len(args),
        out_specs=(anywhere,) * len(results),
        scratch_shapes=[pltpu.VMEM(a.shape, a.dtype) for a in args] + [
            pltpu.VMEM(controls.shape, jnp.float32),
            pltpu.VMEM((rows, LANES), jnp.float32),
            pltpu.VMEM((2, rows, columns), jnp.float32),
            pltpu.VMEM(controls.shape, jnp.float32),
            pltpu.VMEM((2, packed, columns), jnp.float32),
            pltpu.VMEM((2, n_gx, 2, packed, columns), jnp.float32),
            pltpu.VMEM((2, n_gy, n_gz, columns // LANES, 2, rows, LANES), jnp.float32),
            pltpu.VMEM((n_gz, 2, rows, columns), jnp.float32),
            pltpu.VMEM((n_gz, *anomalies.shape), jnp.float32),
            pltpu.VMEM((total, 2, LANES), jnp.float32),
            pltpu.VMEM((obs_cells.shape[-1], columns), jnp.bfloat16),
            pltpu.VMEM((2, columns // LANES, step_count(rows), rows, LANES), jnp.float32),
            pltpu.VMEM((2, columns // LANES, step_count(LANES), rows, LANES), jnp.float32),
            dma((len(args),)), dma((3,)),
            dma((2, 2, n_gx)), dma((2, 2, n_gx)),
            dma((2, n_gy, n_gz)), dma((2, n_gy, n_gz)),
            dma((2, n_gz)), dma((2, n_gz)),
            dma((total,)), dma((total,)),
        ],
        compiler_params=pltpu.CompilerParams(
            collective_id=0, has_side_effects=True, vmem_limit_bytes=VMEM_BYTES
        ),
    )(*args)
    held = (*held, prev_direction)
    outs = (held[0], prev_direction, held[2])
    return pl.pallas_call(
        results_kernel,
        out_shape=tuple(jax.ShapeDtypeStruct(a.shape, a.dtype) for a in outs),
        in_specs=[anywhere] * len(held),
        out_specs=(anywhere,) * len(outs),
        scratch_shapes=[pltpu.VMEM(a.shape, a.dtype) for a in (*held, prev_direction)] + [dma((4,)), dma((3,))],
        compiler_params=pltpu.CompilerParams(vmem_limit_bytes=VMEM_BYTES),
    )(*held)


def solution(mesh):
    in_specs = (
        P("gz", ("grp", "gx"), "gy"),
        P(None, "gz", ("grp", "gx"), "gy"),
        P(("grp", "gx"), "gy"),
        P(("grp", "gx"), "gy"),
        P(("grp", "gx"), "gy", None),
        P(("grp", "gx"), "gy", None),
        P(("grp", "gx"), "gy", None),
        P(("grp", "gx"), "gy", None),
        P("gz", ("grp", "gx"), "gy"),
        P("gz", ("grp", "gx"), "gy"),
    )
    out_specs = (
        P("gz", ("grp", "gx"), "gy"),
        P("gz", ("grp", "gx"), "gy"),
        P(None, ("grp", "gx"), "gy"),
    )
    return jax.shard_map(shards, mesh=mesh, in_specs=in_specs, out_specs=out_specs, check_vma=False)
```

```python
import functools
import math

import jax
import jax.numpy as jnp
from jax import lax
from jax.experimental import pallas as pl
from jax.experimental.pallas import tpu as pltpu
from jax.sharding import PartitionSpec as P

NDIR = 72
LANES = 128
VMEM_BYTES = 63 * 1024 * 1024
MESH = pl.DeviceIdType.MESH


def rolled(values, shift, axis):
    return pltpu.roll(values, shift % values.shape[axis], axis)


def step_count(size):
    return (size - 1).bit_length()


class Line:
    def __init__(self, rates, onward, back, echo):
        self.rates = rates
        self.scales = jnp.sqrt(1.0 - rates * rates)
        self.onward, self.back, self.echo = onward, back, echo


class Filter:
    def __init__(self, rates, axis, ladder):
        self.axis, self.ladder = axis, ladder
        self.size = rates[0].shape[axis]
        self.steps = step_count(self.size)
        place = lax.broadcasted_iota(jnp.int32, rates[0].shape, axis)
        first, last = place == 0, place == self.size - 1

        edges = [jnp.where(first, 0.0, r) for r in rates] + [jnp.where(last, 0.0, r) for r in rates]
        for at, factor in enumerate(edges):
            way, group = divmod(at, len(rates))
            for step in range(self.steps):
                ladder[way, group, step] = factor
                factor = factor * pltpu.roll(factor, self.shift(step, way), axis)
        self.lines = []
        for group, r in enumerate(rates):
            onward = self.run(0, group, jnp.where(first, r, 0.0)[None])
            back = self.run(1, group, jnp.where(last, r, 0.0)[None])
            echo = self.run(1, group, jnp.sqrt(1.0 - r * r) * onward)
            self.lines.append(Line(r, onward[0], back[0], echo[0]))

    def shift(self, step, way):
        return self.size - 2**step if way else 2**step

    def run(self, way, group, values):
        for step in range(self.steps):
            values = values + self.ladder[way, group, step][None] * pltpu.roll(
                values, self.shift(step, way), self.axis + 1)
        return values

    def local(self, group, leading):
        inward = self.run(0, group, leading)
        return inward, self.run(1, group, self.lines[group].scales * inward)


def split_three(values):
    high = values.astype(jnp.bfloat16)
    rest = values - high.astype(jnp.float32)
    middle = rest.astype(jnp.bfloat16)
    low = (rest - middle.astype(jnp.float32)).astype(jnp.bfloat16)
    return jnp.concatenate([high, middle, low], axis=0)


def kernel(
    sizes,
    controls_h, anomalies_h, x_rates_h, y_rates_h, cells_h, codes_h, values_h, weights_h, prev_h,
    gradient_h, ratio_h, increment_h,
    controls, anomalies, x_rates, y_rates, cells, codes, values, weights, prev,
    gradient, ratio, increment, work, enter, slots_x, slots_y, slots_z, slots_a, slots_s, of_column, ladder_x, ladder_y,
    load_sem, store_sem, send_x, recv_x, send_y, recv_y, send_z, recv_z, send_s, recv_s,
):
    n_gx, n_gy, n_gz = sizes
    total = n_gx * n_gy * n_gz
    gx, gy, gz = (lax.axis_index(name) for name in ("gx", "gy", "gz"))
    me = (gx * n_gy + gy) * n_gz + gz
    members, rows, columns = controls.shape
    parts = [slice(at, at + LANES) for at in range(0, columns, LANES)]
    spread = 1.0 / math.sqrt(members * n_gz - 1)

    near = [(lax.rem(gy + b, n_gy), lax.rem(gz + c, n_gz)) for b in range(n_gy) for c in range(n_gz)]

    def each_peer(body):
        def visit(x, others):
            for y, z in others:
                body((x * n_gy + y) * n_gz + z, {"gx": x, "gy": y, "gz": z})

        visit(gx, near[1:])
        if n_gx <= 4:
            for off in range(1, n_gx):
                visit(lax.rem(gx + off, n_gx), near)
        else:
            lax.fori_loop(1, n_gx, lambda off, c: (visit(lax.rem(gx + off, n_gx), near), c)[1], 0)

    barrier = pltpu.get_barrier_semaphore()
    each_peer(lambda index, place: pl.semaphore_signal(
        barrier, inc=1, device_id=place, device_id_type=MESH))

    loads = [
        pltpu.make_async_copy(src, dst, load_sem.at[i])
        for i, (src, dst) in enumerate((
            (x_rates_h, x_rates), (controls_h, controls), (y_rates_h, y_rates),
            (anomalies_h, anomalies), (cells_h, cells), (codes_h, codes), (values_h, values),
            (weights_h, weights), (prev_h, prev)))
    ]
    for load in loads:
        load.start()

    row_at = lax.broadcasted_iota(jnp.int32, (rows, LANES), 0)
    lane_at = lax.broadcasted_iota(jnp.int32, (rows, LANES), 1)

    def pack_rows(blocks, from_row, group):
        tile = jnp.zeros((rows, LANES), jnp.float32)
        for s, block in enumerate(blocks[group * rows:(group + 1) * rows]):
            tile = jnp.where(row_at == s, rolled(block, s - from_row, 0), tile)
        return tile

    def local_x(at, leading, turn, beyond=None):
        line = along_x.lines[at]
        inward, outward = along_x.local(at, leading)
        ends = [inward[k] for k in range(members)] + [line.onward]
        heads = [outward[k] for k in range(members)] + [line.echo]
        for group in range(slots_x.shape[4] // rows):
            here = pl.ds(group * rows, rows)
            end = pack_rows(ends, rows - 1, group)
            head = pack_rows(heads, 0, group)
            if beyond is not None:
                head = head + beyond[at] * end
            slots_x[turn, gx, 0, at, here] = end
            slots_x[turn, gx, 1, at, here] = head
        return outward

    def copy_x(turn, kind, at, source, peer):
        return pltpu.make_async_remote_copy(
            src_ref=slots_x.at[turn, source, kind, at], dst_ref=slots_x.at[turn, source, kind, at],
            send_sem=send_x.at[turn, kind, at, peer], recv_sem=recv_x.at[turn, kind, at, source],
            device_id={"gx": peer}, device_id_type=MESH)

    def outgoing_x(turn, at, act):
        for off in range(1, n_gx):
            peer = lax.rem(gx + off, n_gx)

            @pl.when(gx < n_gx - 1 if turn == 0 else peer > gx)
            def _():
                act(copy_x(turn, 0, at, gx, peer))

            @pl.when(peer < gx)
            def _():
                act(copy_x(turn, 1, at, gx, peer))

    def incoming_x(turn, at):
        for off in range(1, n_gx):
            source = lax.rem(gx + off, n_gx)

            @pl.when(source < n_gx - 1 if turn == 0 else source < gx)
            def _():
                copy_x(turn, 0, at, source, source).wait_recv()

            @pl.when(source > gx)
            def _():
                copy_x(turn, 1, at, source, source).wait_recv()

    def states_x(turn, at):
        state = jnp.zeros((slots_x.shape[4], LANES), jnp.float32)
        states = [state]
        mine = state
        for t in range(n_gx - 1):
            through = slots_x[0, t, 0, at, members:members + 1]
            state = through * state + slots_x[turn, t, 0, at]
            states.append(state)
            mine = jnp.where(gx == t + 1, state, mine)
        return states, mine

    def backward_x(turn, at, states):
        state = jnp.zeros((slots_x.shape[4], LANES), jnp.float32)
        mine = state
        for t in range(n_gx - 1, 0, -1):
            if t < n_gx - 1:
                state = slots_x[0, t, 0, at, members:members + 1] * state
            state = state + slots_x[turn, t, 1, at]
            if states is not None:
                state = state + slots_x[0, t, 1, at, members:members + 1] * states[t]
            mine = jnp.where(gx == t - 1, state, mine)
        return mine

    def response_x(at):
        factor = jnp.zeros((1, LANES), jnp.float32)
        mine = factor
        for t in range(n_gx - 1, 0, -1):
            if t < n_gx - 1:
                through = slots_x[0, t, 0, at, members:members + 1]
                factor = through * through * factor
            factor = factor + slots_x[0, t, 1, at, members:members + 1]
            mine = jnp.where(gx == t - 1, factor, mine)
        return mine

    def finish_x(turn, at, outward, responses=None):
        incoming_x(turn, at)
        part, line = parts[at], along_x.lines[at]
        states, mine = states_x(turn, at)
        enter[0, :, part] = mine
        if responses is None:
            enter[1, :, part] = backward_x(turn, at, states)
        else:
            leaving = slots_x[0, gx, 0, at, members:members + 1] * mine + slots_x[turn, gx, 0, at]
            enter[1, :, part] = backward_x(turn, at, None) + responses[at] * leaving
        for k in range(members):
            first = jnp.broadcast_to(enter[0, k:k + 1, part], (rows, LANES))
            second = jnp.broadcast_to(enter[1, k:k + 1, part], (rows, LANES))
            work[k, :, part] = outward[k] + line.echo * first + line.back * second
        return work[:, :, part]

    def pack_lanes(field, from_lane):
        tile = jnp.zeros((rows, LANES), jnp.float32)
        for k in range(members):
            tile = jnp.where(lane_at == k, rolled(field[k], k - from_lane, 1), tile)
        return tile

    def across(tile, lane):
        return jnp.broadcast_to(tile[:, lane:lane + 1], (rows, LANES))

    def local_y(s, leading, turn):
        line = along_y.lines[s]
        inward, outward = along_y.local(s, leading)
        slots_y[turn, gy, gz, s, 0] = jnp.where(
            lane_at == members, across(line.onward, LANES - 1), pack_lanes(inward, LANES - 1))
        slots_y[turn, gy, gz, s, 1] = jnp.where(
            lane_at == members, across(line.echo, 0), pack_lanes(outward, 0))
        return outward

    def each_y(turn, act):
        for y, z in near[1:] if turn == 0 else [near[b * n_gz] for b in range(1, n_gy)]:
            act(y, z)

    def copy_y(turn, source, peer):
        slot = (turn, *source)
        return pltpu.make_async_remote_copy(
            src_ref=slots_y.at[slot], dst_ref=slots_y.at[slot],
            send_sem=send_y.at[turn, *peer], recv_sem=recv_y.at[turn, *source],
            device_id={"gy": peer[0], "gz": peer[1]}, device_id_type=MESH)

    def start_y(turn):
        each_y(turn, lambda *peer: copy_y(turn, (gy, gz), peer).start())

    def entering_y(turn, z):
        chain = [(t, s) for t in range(n_gy) for s in range(len(parts))]
        state = jnp.zeros((rows, LANES), jnp.float32)
        states = []
        firsts = [state] * len(parts)
        for t, s in chain:
            states.append(state)
            firsts[s] = state if t == 0 else jnp.where(gy == t, state, firsts[s])
            tile = slots_y[turn, t, z, s, 0]
            state = across(tile, members) * state + tile
        state = jnp.zeros((rows, LANES), jnp.float32)
        seconds = [state] * len(parts)
        for (t, s), entered in reversed(list(zip(chain, states))):
            seconds[s] = state if t == n_gy - 1 else jnp.where(gy == t, state, seconds[s])
            tile = slots_y[turn, t, z, s, 1]
            state = across(slots_y[turn, t, z, s, 0], members) * state + tile + across(tile, members) * entered
        return firsts, seconds

    def copy_z(source, peer):
        return pltpu.make_async_remote_copy(
            src_ref=slots_z.at[source], dst_ref=slots_z.at[source],
            send_sem=send_z.at[0, peer], recv_sem=recv_z.at[0, source],
            device_id={"gz": peer}, device_id_type=MESH)

    def copy_a(source, peer):
        return pltpu.make_async_remote_copy(
            src_ref=slots_a.at[source], dst_ref=slots_a.at[source],
            send_sem=send_z.at[1, peer], recv_sem=recv_z.at[1, source],
            device_id={"gz": peer}, device_id_type=MESH)

    other_z = [lax.rem(gz + off, n_gz) for off in range(1, n_gz)]

    loads[0].wait()
    along_x = Filter([x_rates[:, part] for part in parts], 0, ladder_x)
    lines_x = along_x.lines
    loads[1].wait()
    outs_x = []
    for at, (part, line) in enumerate(zip(parts, lines_x)):
        outs_x.append(local_x(at, line.scales * controls[:, :, part], 0))
        if at == 0:
            pl.semaphore_wait(barrier, total - 1)
        outgoing_x(0, at, lambda copy: copy.start())

    loads[2].wait()
    along_y = Filter([y_rates[:, part] for part in parts], 1, ladder_y)
    lines_y = along_y.lines
    for load in loads[3:]:
        load.wait()
    slots_a[gz] = anomalies[...].astype(jnp.float32)
    for z in other_z:
        copy_a(gz, z).start()
    n_obs = cells.shape[-1]
    cell = cells[0]
    bits = columns.bit_length() - 1
    cell_row = lax.shift_right_logical(cell, jnp.full_like(cell, bits))
    cell_column = cell & (columns - 1)
    bearing = codes[0].astype(jnp.float32) * (2.0 * math.pi / NDIR)
    cosine = jnp.cos(bearing)
    sine = jnp.sin(bearing)
    hit = (lax.broadcasted_iota(jnp.int32, (columns, n_obs), 0) == cell_column).astype(jnp.float32)
    at_column = hit.astype(jnp.bfloat16)
    of_column[...] = hit.T.astype(jnp.bfloat16)
    in_row = lax.broadcasted_iota(jnp.int32, (rows, n_obs), 0) == cell_row
    toward = jnp.concatenate([jnp.where(in_row, cosine, 0.0), jnp.where(in_row, sine, 0.0)], axis=0)
    before = prev[...]
    denominator = jnp.sum(jnp.sum(before * before, axis=0), axis=0, keepdims=True)

    outs = [
        local_y(at, line.scales * finish_x(0, at, outs_x[at]), 0) for at, line in enumerate(lines_y)]
    start_y(0)
    for c in range(2):
        for part, field in zip(parts, outs):
            slots_z[gz, c, :, part] = jnp.sum(slots_a[gz, c, :, :, part] * field, axis=0)
    for z in other_z:
        copy_z(gz, z).start()
    responses = [response_x(at) for at in range(len(parts))]
    beyond = [line.onward[rows - 1:] * response for line, response in zip(lines_x, responses)]
    for z in other_z:
        copy_a(z, z).wait_recv()
    each_y(0, lambda *source: copy_y(0, source, source).wait_recv())
    for z in other_z:
        copy_z(z, z).wait_recv()
    for z in range(n_gz):
        firsts, seconds = entering_y(0, z)
        for s, (part, line) in enumerate(zip(parts, lines_y)):
            sums = [[jnp.zeros((rows, LANES), jnp.float32)] * 2 for _ in range(2)]
            for k in range(members):
                for e, state in enumerate((across(firsts[s], k), across(seconds[s], k))):
                    for c in range(2):
                        sums[c][e] = sums[c][e] + slots_a[z, c, k, :, part] * state
            for c in range(2):
                share = slots_z[z, c, :, part] + line.echo * sums[c][0] + line.back * sums[c][1]
                increment[c, :, part] = share if z == 0 else increment[c, :, part] + share
    grown = increment[...] * spread
    increment[...] = grown
    store_increment = pltpu.make_async_copy(increment, increment_h, store_sem.at[0])
    store_increment.start()

    lifted = jnp.dot(
        split_three(jnp.concatenate([grown[0], grown[1]], axis=0)), at_column,
        preferred_element_type=jnp.float32)
    lifted = lifted[:2 * rows] + (lifted[2 * rows:4 * rows] + lifted[4 * rows:])
    projected = jnp.sum(lifted * toward, axis=0, keepdims=True)
    misfit = weights[0] * (projected - values[0])
    back = jnp.dot(
        split_three(toward * misfit), of_column[...], preferred_element_type=jnp.float32)
    back = (back[:2 * rows] + (back[2 * rows:4 * rows] + back[4 * rows:])) * spread

    outs = []
    for s, (part, line) in enumerate(zip(parts, lines_y)):
        pulled = (slots_a[gz, 0, :, :, part] * back[None, :rows, part]
                  + slots_a[gz, 1, :, :, part] * back[None, rows:, part])
        outs.append(local_y(s, line.rates * pulled, 1))
    start_y(1)
    each_y(1, lambda *source: copy_y(1, source, source).wait_recv())
    firsts, seconds = entering_y(1, gz)
    outs_x = []
    for s, (part, line_x, line_y) in enumerate(zip(parts, lines_x, lines_y)):
        scale = line_y.scales / line_y.rates * line_x.rates
        echo, after = scale * line_y.echo, scale * line_y.back
        for k in range(members):
            work[k, :, part] = scale * outs[s][k] + echo * across(firsts[s], k) + after * across(seconds[s], k)
        outs_x.append(local_x(s, work[:, :, part], 1, beyond))
        outgoing_x(1, s, lambda copy: copy.start())
    numerator = jnp.zeros((rows, LANES), jnp.float32)
    for at, (part, line) in enumerate(zip(parts, lines_x)):
        field = finish_x(1, at, outs_x[at], responses)
        new = controls[:, :, part] + line.scales / line.rates * field
        gradient[:, :, part] = new
        numerator = numerator + jnp.sum(new * (new - prev[:, :, part]), axis=0)
    store_gradient = pltpu.make_async_copy(gradient, gradient_h, store_sem.at[1])
    store_gradient.start()

    halves = denominator[:, parts[0]]
    for part in parts[1:]:
        halves = halves + denominator[:, part]
    slots_s[me, 0:1] = jnp.sum(numerator, axis=0, keepdims=True)
    slots_s[me, 1:2] = halves

    def copy_s(source, peer, place):
        return pltpu.make_async_remote_copy(
            src_ref=slots_s.at[source], dst_ref=slots_s.at[source],
            send_sem=send_s.at[peer], recv_sem=recv_s.at[source],
            device_id=place, device_id_type=MESH)

    each_peer(lambda peer, place: copy_s(me, peer, place).start())
    each_peer(lambda peer, place: copy_s(peer, peer, place).wait_recv())
    sums = jnp.sum(jnp.sum(slots_s[...], axis=0), axis=1, keepdims=True)
    ratio[...] = jnp.broadcast_to(sums[0:1] / sums[1:2], ratio.shape)
    store_ratio = pltpu.make_async_copy(ratio, ratio_h, store_sem.at[2])
    store_ratio.start()

    each_peer(lambda peer, place: copy_s(me, peer, place).wait_send())
    for turn in range(2):
        for at in range(len(parts)):
            outgoing_x(turn, at, lambda copy: copy.wait_send())
        each_y(turn, lambda *peer: copy_y(turn, (gy, gz), peer).wait_send())
    for z in other_z:
        copy_z(gz, z).wait_send()
        copy_a(gz, z).wait_send()
    store_increment.wait()
    store_gradient.wait()
    store_ratio.wait()


def results_kernel(
    gradient_h, ratio_h, increment_h, old_h, gradient_out, direction_out, increment_out,
    gradient, ratio, increment, old, direction, load_sem, store_sem,
):
    loads = [
        pltpu.make_async_copy(src, dst, load_sem.at[i])
        for i, (src, dst) in enumerate((
            (ratio_h, ratio), (gradient_h, gradient), (old_h, old), (increment_h, increment)))
    ]
    stores = [
        pltpu.make_async_copy(src, dst, store_sem.at[i])
        for i, (src, dst) in enumerate((
            (gradient, gradient_out), (direction, direction_out), (increment, increment_out)))
    ]
    for load in loads:
        load.start()
    loads[0].wait()
    loads[1].wait()
    stores[0].start()
    loads[2].wait()
    for at in range(0, gradient.shape[2], LANES):
        part = slice(at, at + LANES)
        direction[:, :, part] = ratio[...][None] * old[:, :, part] - gradient[:, :, part]
    stores[1].start()
    loads[3].wait()
    stores[2].start()
    for store in stores:
        store.wait()


def shards(
    controls,
    anomalies,
    x_rates,
    y_rates,
    obs_cells,
    obs_codes,
    obs_values,
    obs_weights,
    prev_gradient,
    prev_direction,
):
    n_gx, n_gy, n_gz = (lax.axis_size(name) for name in ("gx", "gy", "gz"))
    total = n_gx * n_gy * n_gz
    members, rows, columns = controls.shape
    packed = -(-(members + 1) // rows) * rows
    args = (controls, anomalies, x_rates, y_rates, obs_cells, obs_codes, obs_values, obs_weights, prev_gradient)
    dma = pltpu.SemaphoreType.DMA
    anywhere = pl.BlockSpec(memory_space=pl.ANY)
    results = tuple(
        jax.ShapeDtypeStruct(shape, jnp.float32)
        for shape in (controls.shape, (rows, LANES), (2, rows, columns)))
    held = pl.pallas_call(
        functools.partial(kernel, (n_gx, n_gy, n_gz)),
        out_shape=results,
        in_specs=[anywhere] * len(args),
        out_specs=(anywhere,) * len(results),
        scratch_shapes=[pltpu.VMEM(a.shape, a.dtype) for a in args] + [
            pltpu.VMEM(controls.shape, jnp.float32),
            pltpu.VMEM((rows, LANES), jnp.float32),
            pltpu.VMEM((2, rows, columns), jnp.float32),
            pltpu.VMEM(controls.shape, jnp.float32),
            pltpu.VMEM((2, packed, columns), jnp.float32),
            pltpu.VMEM((2, n_gx, 2, columns // LANES, packed, LANES), jnp.float32),
            pltpu.VMEM((2, n_gy, n_gz, columns // LANES, 2, rows, LANES), jnp.float32),
            pltpu.VMEM((n_gz, 2, rows, columns), jnp.float32),
            pltpu.VMEM((n_gz, *anomalies.shape), jnp.float32),
            pltpu.VMEM((total, 2, LANES), jnp.float32),
            pltpu.VMEM((obs_cells.shape[-1], columns), jnp.bfloat16),
            pltpu.VMEM((2, columns // LANES, step_count(rows), rows, LANES), jnp.float32),
            pltpu.VMEM((2, columns // LANES, step_count(LANES), rows, LANES), jnp.float32),
            dma((len(args),)), dma((3,)),
            dma((2, 2, columns // LANES, n_gx)), dma((2, 2, columns // LANES, n_gx)),
            dma((2, n_gy, n_gz)), dma((2, n_gy, n_gz)),
            dma((2, n_gz)), dma((2, n_gz)),
            dma((total,)), dma((total,)),
        ],
        compiler_params=pltpu.CompilerParams(
            collective_id=0, has_side_effects=True, vmem_limit_bytes=VMEM_BYTES
        ),
    )(*args)
    held = (*held, prev_direction)
    outs = (held[0], prev_direction, held[2])
    return pl.pallas_call(
        results_kernel,
        out_shape=tuple(jax.ShapeDtypeStruct(a.shape, a.dtype) for a in outs),
        in_specs=[anywhere] * len(held),
        out_specs=(anywhere,) * len(outs),
        scratch_shapes=[pltpu.VMEM(a.shape, a.dtype) for a in (*held, prev_direction)] + [dma((4,)), dma((3,))],
        compiler_params=pltpu.CompilerParams(vmem_limit_bytes=VMEM_BYTES),
    )(*held)


def solution(mesh):
    in_specs = (
        P("gz", ("grp", "gx"), "gy"),
        P(None, "gz", ("grp", "gx"), "gy"),
        P(("grp", "gx"), "gy"),
        P(("grp", "gx"), "gy"),
        P(("grp", "gx"), "gy", None),
        P(("grp", "gx"), "gy", None),
        P(("grp", "gx"), "gy", None),
        P(("grp", "gx"), "gy", None),
        P("gz", ("grp", "gx"), "gy"),
        P("gz", ("grp", "gx"), "gy"),
    )
    out_specs = (
        P("gz", ("grp", "gx"), "gy"),
        P("gz", ("grp", "gx"), "gy"),
        P(None, ("grp", "gx"), "gy"),
    )
    return jax.shard_map(shards, mesh=mesh, in_specs=in_specs, out_specs=out_specs, check_vma=False)
```

```python
import functools
import math

import jax
import jax.numpy as jnp
from jax import lax
from jax.experimental import pallas as pl
from jax.experimental.pallas import tpu as pltpu
from jax.sharding import PartitionSpec as P

NDIR = 72
LANES = 128
VMEM_BYTES = 63 * 1024 * 1024
MESH = pl.DeviceIdType.MESH


def rolled(values, shift, axis):
    return pltpu.roll(values, shift % values.shape[axis], axis)


def step_count(size):
    return (size - 1).bit_length()


class Line:
    def __init__(self, rates, onward, back, echo):
        self.rates = rates
        self.scales = jnp.sqrt(1.0 - rates * rates)
        self.onward, self.back, self.echo = onward, back, echo


class Filter:
    def __init__(self, rates, axis, ladder):
        self.axis, self.ladder = axis, ladder
        self.size = rates[0].shape[axis]
        self.steps = step_count(self.size)
        place = lax.broadcasted_iota(jnp.int32, rates[0].shape, axis)
        first, last = place == 0, place == self.size - 1

        edges = [jnp.where(first, 0.0, r) for r in rates] + [jnp.where(last, 0.0, r) for r in rates]
        for at, factor in enumerate(edges):
            way, group = divmod(at, len(rates))
            for step in range(self.steps):
                ladder[way, group, step] = factor
                factor = factor * pltpu.roll(factor, self.shift(step, way), axis)
        self.lines = []
        for group, r in enumerate(rates):
            onward = self.run(0, group, jnp.where(first, r, 0.0)[None])
            back = self.run(1, group, jnp.where(last, r, 0.0)[None])
            echo = self.run(1, group, jnp.sqrt(1.0 - r * r) * onward)
            self.lines.append(Line(r, onward[0], back[0], echo[0]))

    def shift(self, step, way):
        return self.size - 2**step if way else 2**step

    def run(self, way, group, values):
        for step in range(self.steps):
            values = values + self.ladder[way, group, step][None] * pltpu.roll(
                values, self.shift(step, way), self.axis + 1)
        return values

    def local(self, group, leading):
        inward = self.run(0, group, leading)
        return inward, self.run(1, group, self.lines[group].scales * inward)


def split_three(values):
    high = values.astype(jnp.bfloat16)
    rest = values - high.astype(jnp.float32)
    middle = rest.astype(jnp.bfloat16)
    low = (rest - middle.astype(jnp.float32)).astype(jnp.bfloat16)
    return jnp.concatenate([high, middle, low], axis=0)


def kernel(
    sizes,
    controls_h, anomalies_h, x_rates_h, y_rates_h, cells_h, codes_h, values_h, weights_h, prev_h,
    gradient_h, ratio_h, increment_h,
    controls, anomalies, x_rates, y_rates, cells, codes, values, weights, prev,
    gradient, ratio, increment, work, enter, slots_x, slots_y, slots_z, slots_a, slots_s, of_column, ladder_x, ladder_y,
    load_sem, store_sem, send_x, recv_x, send_y, recv_y, send_z, recv_z, send_s, recv_s,
):
    n_gx, n_gy, n_gz = sizes
    total = n_gx * n_gy * n_gz
    gx, gy, gz = (lax.axis_index(name) for name in ("gx", "gy", "gz"))
    me = (gx * n_gy + gy) * n_gz + gz
    members, rows, columns = controls.shape
    parts = [slice(at, at + LANES) for at in range(0, columns, LANES)]
    spread = 1.0 / math.sqrt(members * n_gz - 1)

    near = [(lax.rem(gy + b, n_gy), lax.rem(gz + c, n_gz)) for b in range(n_gy) for c in range(n_gz)]

    def each_peer(body):
        def visit(x, others):
            for y, z in others:
                body((x * n_gy + y) * n_gz + z, {"gx": x, "gy": y, "gz": z})

        visit(gx, near[1:])
        if n_gx <= 4:
            for off in range(1, n_gx):
                visit(lax.rem(gx + off, n_gx), near)
        else:
            lax.fori_loop(1, n_gx, lambda off, c: (visit(lax.rem(gx + off, n_gx), near), c)[1], 0)

    barrier = pltpu.get_barrier_semaphore()
    each_peer(lambda index, place: pl.semaphore_signal(
        barrier, inc=1, device_id=place, device_id_type=MESH))

    loads = [
        pltpu.make_async_copy(src, dst, load_sem.at[i])
        for i, (src, dst) in enumerate((
            (x_rates_h, x_rates), (controls_h, controls), (y_rates_h, y_rates),
            (anomalies_h, anomalies), (cells_h, cells), (codes_h, codes), (values_h, values),
            (weights_h, weights), (prev_h, prev)))
    ]
    for load in loads:
        load.start()

    row_at = lax.broadcasted_iota(jnp.int32, (rows, LANES), 0)
    lane_at = lax.broadcasted_iota(jnp.int32, (rows, LANES), 1)

    def pack_rows(blocks, from_row, group):
        tile = jnp.zeros((rows, LANES), jnp.float32)
        for s, block in enumerate(blocks[group * rows:(group + 1) * rows]):
            tile = jnp.where(row_at == s, rolled(block, s - from_row, 0), tile)
        return tile

    def local_x(at, leading, turn, beyond=None):
        line = along_x.lines[at]
        inward, outward = along_x.local(at, leading)
        ends = [inward[k] for k in range(members)] + [line.onward]
        heads = [outward[k] for k in range(members)] + [line.echo]
        for group in range(slots_x.shape[4] // rows):
            here = pl.ds(group * rows, rows)
            end = pack_rows(ends, rows - 1, group)
            head = pack_rows(heads, 0, group)
            if beyond is not None:
                head = head + beyond[at] * end
            slots_x[turn, gx, 0, at, here] = end
            slots_x[turn, gx, 1, at, here] = head
        return outward

    def copy_x(turn, source, peer, leftward):
        slot = (turn, source) if leftward and turn == 0 else (turn, source, 1 if leftward else 0)
        return pltpu.make_async_remote_copy(
            src_ref=slots_x.at[slot], dst_ref=slots_x.at[slot],
            send_sem=send_x.at[turn, peer], recv_sem=recv_x.at[turn, source],
            device_id={"gx": peer}, device_id_type=MESH)

    def outgoing_x(turn, act):
        for off in range(1, n_gx):
            peer = lax.rem(gx + off, n_gx)
            pl.when(peer > gx)(lambda: act(copy_x(turn, gx, peer, False)))
            pl.when(peer < gx)(lambda: act(copy_x(turn, gx, peer, True)))

    def incoming_x(turn):
        for off in range(1, n_gx):
            source = lax.rem(gx + off, n_gx)
            pl.when(source < gx)(lambda: copy_x(turn, source, source, False).wait_recv())
            pl.when(source > gx)(lambda: copy_x(turn, source, source, True).wait_recv())

    def states_x(turn, at):
        state = jnp.zeros((slots_x.shape[4], LANES), jnp.float32)
        states = [state]
        mine = state
        for t in range(n_gx - 1):
            through = slots_x[0, t, 0, at, members:members + 1]
            state = through * state + slots_x[turn, t, 0, at]
            states.append(state)
            mine = jnp.where(gx == t + 1, state, mine)
        return states, mine

    def backward_x(turn, at, states):
        state = jnp.zeros((slots_x.shape[4], LANES), jnp.float32)
        mine = state
        for t in range(n_gx - 1, 0, -1):
            if t < n_gx - 1:
                state = slots_x[0, t, 0, at, members:members + 1] * state
            state = state + slots_x[turn, t, 1, at]
            if states is not None:
                state = state + slots_x[0, t, 1, at, members:members + 1] * states[t]
            mine = jnp.where(gx == t - 1, state, mine)
        return mine

    def response_x(at):
        factor = jnp.zeros((1, LANES), jnp.float32)
        mine = factor
        for t in range(n_gx - 1, 0, -1):
            if t < n_gx - 1:
                through = slots_x[0, t, 0, at, members:members + 1]
                factor = through * through * factor
            factor = factor + slots_x[0, t, 1, at, members:members + 1]
            mine = jnp.where(gx == t - 1, factor, mine)
        return mine

    def finish_x(turn, at, outward, responses=None):
        part, line = parts[at], along_x.lines[at]
        states, mine = states_x(turn, at)
        enter[0, :, part] = mine
        if responses is None:
            enter[1, :, part] = backward_x(turn, at, states)
        else:
            leaving = slots_x[0, gx, 0, at, members:members + 1] * mine + slots_x[turn, gx, 0, at]
            enter[1, :, part] = backward_x(turn, at, None) + responses[at] * leaving
        for k in range(members):
            first = jnp.broadcast_to(enter[0, k:k + 1, part], (rows, LANES))
            second = jnp.broadcast_to(enter[1, k:k + 1, part], (rows, LANES))
            work[k, :, part] = outward[k] + line.echo * first + line.back * second
        return work[:, :, part]

    def pack_lanes(field, from_lane):
        tile = jnp.zeros((rows, LANES), jnp.float32)
        for k in range(members):
            tile = jnp.where(lane_at == k, rolled(field[k], k - from_lane, 1), tile)
        return tile

    def across(tile, lane):
        return jnp.broadcast_to(tile[:, lane:lane + 1], (rows, LANES))

    def local_y(s, leading, turn):
        line = along_y.lines[s]
        inward, outward = along_y.local(s, leading)
        slots_y[turn, gy, gz, s, 0] = jnp.where(
            lane_at == members, across(line.onward, LANES - 1), pack_lanes(inward, LANES - 1))
        slots_y[turn, gy, gz, s, 1] = jnp.where(
            lane_at == members, across(line.echo, 0), pack_lanes(outward, 0))
        return outward

    def each_y(turn, act):
        for y, z in near[1:] if turn == 0 else [near[b * n_gz] for b in range(1, n_gy)]:
            act(y, z)

    def copy_y(turn, source, peer):
        slot = (turn, *source)
        return pltpu.make_async_remote_copy(
            src_ref=slots_y.at[slot], dst_ref=slots_y.at[slot],
            send_sem=send_y.at[turn, *peer], recv_sem=recv_y.at[turn, *source],
            device_id={"gy": peer[0], "gz": peer[1]}, device_id_type=MESH)

    def start_y(turn):
        each_y(turn, lambda *peer: copy_y(turn, (gy, gz), peer).start())

    def entering_y(turn, z):
        chain = [(t, s) for t in range(n_gy) for s in range(len(parts))]
        state = jnp.zeros((rows, LANES), jnp.float32)
        states = []
        firsts = [state] * len(parts)
        for t, s in chain:
            states.append(state)
            firsts[s] = state if t == 0 else jnp.where(gy == t, state, firsts[s])
            tile = slots_y[turn, t, z, s, 0]
            state = across(tile, members) * state + tile
        state = jnp.zeros((rows, LANES), jnp.float32)
        seconds = [state] * len(parts)
        for (t, s), entered in reversed(list(zip(chain, states))):
            seconds[s] = state if t == n_gy - 1 else jnp.where(gy == t, state, seconds[s])
            tile = slots_y[turn, t, z, s, 1]
            state = across(slots_y[turn, t, z, s, 0], members) * state + tile + across(tile, members) * entered
        return firsts, seconds

    def copy_z(source, peer):
        return pltpu.make_async_remote_copy(
            src_ref=slots_z.at[source], dst_ref=slots_z.at[source],
            send_sem=send_z.at[0, peer], recv_sem=recv_z.at[0, source],
            device_id={"gz": peer}, device_id_type=MESH)

    def copy_a(source, peer):
        return pltpu.make_async_remote_copy(
            src_ref=slots_a.at[source], dst_ref=slots_a.at[source],
            send_sem=send_z.at[1, peer], recv_sem=recv_z.at[1, source],
            device_id={"gz": peer}, device_id_type=MESH)

    other_z = [lax.rem(gz + off, n_gz) for off in range(1, n_gz)]

    loads[0].wait()
    along_x = Filter([x_rates[:, part] for part in parts], 0, ladder_x)
    lines_x = along_x.lines
    loads[1].wait()
    outs_x = []
    for at, (part, line) in enumerate(zip(parts, lines_x)):
        outs_x.append(local_x(at, line.scales * controls[:, :, part], 0))
    pl.semaphore_wait(barrier, total - 1)
    outgoing_x(0, lambda copy: copy.start())

    loads[2].wait()
    along_y = Filter([y_rates[:, part] for part in parts], 1, ladder_y)
    lines_y = along_y.lines
    for load in loads[3:]:
        load.wait()
    slots_a[gz] = anomalies[...].astype(jnp.float32)
    for z in other_z:
        copy_a(gz, z).start()
    n_obs = cells.shape[-1]
    cell = cells[0]
    bits = columns.bit_length() - 1
    cell_row = lax.shift_right_logical(cell, jnp.full_like(cell, bits))
    cell_column = cell & (columns - 1)
    bearing = codes[0].astype(jnp.float32) * (2.0 * math.pi / NDIR)
    cosine = jnp.cos(bearing)
    sine = jnp.sin(bearing)
    hit = (lax.broadcasted_iota(jnp.int32, (columns, n_obs), 0) == cell_column).astype(jnp.float32)
    at_column = hit.astype(jnp.bfloat16)
    of_column[...] = hit.T.astype(jnp.bfloat16)
    in_row = lax.broadcasted_iota(jnp.int32, (rows, n_obs), 0) == cell_row
    toward = jnp.concatenate([jnp.where(in_row, cosine, 0.0), jnp.where(in_row, sine, 0.0)], axis=0)
    before = prev[...]
    denominator = jnp.sum(jnp.sum(before * before, axis=0), axis=0, keepdims=True)

    incoming_x(0)
    outs = [
        local_y(at, line.scales * finish_x(0, at, outs_x[at]), 0) for at, line in enumerate(lines_y)]
    start_y(0)
    for c in range(2):
        for part, field in zip(parts, outs):
            slots_z[gz, c, :, part] = jnp.sum(slots_a[gz, c, :, :, part] * field, axis=0)
    for z in other_z:
        copy_z(gz, z).start()
    responses = [response_x(at) for at in range(len(parts))]
    beyond = [line.onward[rows - 1:] * response for line, response in zip(lines_x, responses)]
    for z in other_z:
        copy_a(z, z).wait_recv()
    each_y(0, lambda *source: copy_y(0, source, source).wait_recv())
    for z in other_z:
        copy_z(z, z).wait_recv()
    for z in range(n_gz):
        firsts, seconds = entering_y(0, z)
        for s, (part, line) in enumerate(zip(parts, lines_y)):
            sums = [[jnp.zeros((rows, LANES), jnp.float32)] * 2 for _ in range(2)]
            for k in range(members):
                for e, state in enumerate((across(firsts[s], k), across(seconds[s], k))):
                    for c in range(2):
                        sums[c][e] = sums[c][e] + slots_a[z, c, k, :, part] * state
            for c in range(2):
                share = slots_z[z, c, :, part] + line.echo * sums[c][0] + line.back * sums[c][1]
                increment[c, :, part] = share if z == 0 else increment[c, :, part] + share
    grown = increment[...] * spread
    increment[...] = grown
    store_increment = pltpu.make_async_copy(increment, increment_h, store_sem.at[0])
    store_increment.start()

    lifted = jnp.dot(
        split_three(jnp.concatenate([grown[0], grown[1]], axis=0)), at_column,
        preferred_element_type=jnp.float32)
    lifted = lifted[:2 * rows] + (lifted[2 * rows:4 * rows] + lifted[4 * rows:])
    projected = jnp.sum(lifted * toward, axis=0, keepdims=True)
    misfit = weights[0] * (projected - values[0])
    back = jnp.dot(
        split_three(toward * misfit), of_column[...], preferred_element_type=jnp.float32)
    back = (back[:2 * rows] + (back[2 * rows:4 * rows] + back[4 * rows:])) * spread

    outs = []
    for s, (part, line) in enumerate(zip(parts, lines_y)):
        pulled = (slots_a[gz, 0, :, :, part] * back[None, :rows, part]
                  + slots_a[gz, 1, :, :, part] * back[None, rows:, part])
        outs.append(local_y(s, line.rates * pulled, 1))
    start_y(1)
    each_y(1, lambda *source: copy_y(1, source, source).wait_recv())
    firsts, seconds = entering_y(1, gz)
    outs_x = []
    for s, (part, line_x, line_y) in enumerate(zip(parts, lines_x, lines_y)):
        scale = line_y.scales / line_y.rates * line_x.rates
        echo, after = scale * line_y.echo, scale * line_y.back
        for k in range(members):
            work[k, :, part] = scale * outs[s][k] + echo * across(firsts[s], k) + after * across(seconds[s], k)
        outs_x.append(local_x(s, work[:, :, part], 1, beyond))
    outgoing_x(1, lambda copy: copy.start())
    incoming_x(1)
    numerator = jnp.zeros((rows, LANES), jnp.float32)
    for at, (part, line) in enumerate(zip(parts, lines_x)):
        field = finish_x(1, at, outs_x[at], responses)
        new = controls[:, :, part] + line.scales / line.rates * field
        gradient[:, :, part] = new
        numerator = numerator + jnp.sum(new * (new - prev[:, :, part]), axis=0)
    store_gradient = pltpu.make_async_copy(gradient, gradient_h, store_sem.at[1])
    store_gradient.start()

    halves = denominator[:, parts[0]]
    for part in parts[1:]:
        halves = halves + denominator[:, part]
    slots_s[me, 0:1] = jnp.sum(numerator, axis=0, keepdims=True)
    slots_s[me, 1:2] = halves

    def copy_s(source, peer, place):
        return pltpu.make_async_remote_copy(
            src_ref=slots_s.at[source], dst_ref=slots_s.at[source],
            send_sem=send_s.at[0], recv_sem=recv_s.at[0],
            device_id=place, device_id_type=MESH)

    each_peer(lambda peer, place: copy_s(me, peer, place).start())
    for turn in range(2):
        outgoing_x(turn, lambda copy: copy.wait_send())
        each_y(turn, lambda *peer: copy_y(turn, (gy, gz), peer).wait_send())
    for z in other_z:
        copy_z(gz, z).wait_send()
        copy_a(gz, z).wait_send()
    store_increment.wait()
    others = slots_s.at[pl.ds(0, total - 1)]
    all_s = pltpu.make_async_remote_copy(
        src_ref=others, dst_ref=others, send_sem=send_s.at[0], recv_sem=recv_s.at[0],
        device_id={"gx": lax.rem(gx + 1, n_gx)}, device_id_type=MESH)
    all_s.wait_recv()
    sums = jnp.sum(jnp.sum(slots_s[...], axis=0), axis=1, keepdims=True)
    ratio[...] = jnp.broadcast_to(sums[0:1] / sums[1:2], ratio.shape)
    store_ratio = pltpu.make_async_copy(ratio, ratio_h, store_sem.at[2])
    store_ratio.start()

    all_s.wait_send()
    store_gradient.wait()
    store_ratio.wait()


def results_kernel(
    gradient_h, ratio_h, increment_h, old_h, gradient_out, direction_out, increment_out,
    gradient, ratio, increment, old, direction, load_sem, store_sem,
):
    loads = [
        pltpu.make_async_copy(src, dst, load_sem.at[i])
        for i, (src, dst) in enumerate((
            (ratio_h, ratio), (gradient_h, gradient), (old_h, old), (increment_h, increment)))
    ]
    stores = [
        pltpu.make_async_copy(src, dst, store_sem.at[i])
        for i, (src, dst) in enumerate((
            (gradient, gradient_out), (direction, direction_out), (increment, increment_out)))
    ]
    for load in loads:
        load.start()
    loads[0].wait()
    loads[1].wait()
    stores[0].start()
    loads[2].wait()
    for at in range(0, gradient.shape[2], LANES):
        part = slice(at, at + LANES)
        direction[:, :, part] = ratio[...][None] * old[:, :, part] - gradient[:, :, part]
    stores[1].start()
    loads[3].wait()
    stores[2].start()
    for store in stores:
        store.wait()


def shards(
    controls,
    anomalies,
    x_rates,
    y_rates,
    obs_cells,
    obs_codes,
    obs_values,
    obs_weights,
    prev_gradient,
    prev_direction,
):
    n_gx, n_gy, n_gz = (lax.axis_size(name) for name in ("gx", "gy", "gz"))
    total = n_gx * n_gy * n_gz
    members, rows, columns = controls.shape
    packed = -(-(members + 1) // rows) * rows
    args = (controls, anomalies, x_rates, y_rates, obs_cells, obs_codes, obs_values, obs_weights, prev_gradient)
    dma = pltpu.SemaphoreType.DMA
    anywhere = pl.BlockSpec(memory_space=pl.ANY)
    results = tuple(
        jax.ShapeDtypeStruct(shape, jnp.float32)
        for shape in (controls.shape, (rows, LANES), (2, rows, columns)))
    held = pl.pallas_call(
        functools.partial(kernel, (n_gx, n_gy, n_gz)),
        out_shape=results,
        in_specs=[anywhere] * len(args),
        out_specs=(anywhere,) * len(results),
        scratch_shapes=[pltpu.VMEM(a.shape, a.dtype) for a in args] + [
            pltpu.VMEM(controls.shape, jnp.float32),
            pltpu.VMEM((rows, LANES), jnp.float32),
            pltpu.VMEM((2, rows, columns), jnp.float32),
            pltpu.VMEM(controls.shape, jnp.float32),
            pltpu.VMEM((2, packed, columns), jnp.float32),
            pltpu.VMEM((2, n_gx, 2, columns // LANES, packed, LANES), jnp.float32),
            pltpu.VMEM((2, n_gy, n_gz, columns // LANES, 2, rows, LANES), jnp.float32),
            pltpu.VMEM((n_gz, 2, rows, columns), jnp.float32),
            pltpu.VMEM((n_gz, *anomalies.shape), jnp.float32),
            pltpu.VMEM((total, 2, LANES), jnp.float32),
            pltpu.VMEM((obs_cells.shape[-1], columns), jnp.bfloat16),
            pltpu.VMEM((2, columns // LANES, step_count(rows), rows, LANES), jnp.float32),
            pltpu.VMEM((2, columns // LANES, step_count(LANES), rows, LANES), jnp.float32),
            dma((len(args),)), dma((3,)),
            dma((2, n_gx)), dma((2, n_gx)),
            dma((2, n_gy, n_gz)), dma((2, n_gy, n_gz)),
            dma((2, n_gz)), dma((2, n_gz)),
            dma((1,)), dma((1,)),
        ],
        compiler_params=pltpu.CompilerParams(
            collective_id=0, has_side_effects=True, vmem_limit_bytes=VMEM_BYTES
        ),
    )(*args)
    held = (*held, prev_direction)
    outs = (held[0], prev_direction, held[2])
    return pl.pallas_call(
        results_kernel,
        out_shape=tuple(jax.ShapeDtypeStruct(a.shape, a.dtype) for a in outs),
        in_specs=[anywhere] * len(held),
        out_specs=(anywhere,) * len(outs),
        scratch_shapes=[pltpu.VMEM(a.shape, a.dtype) for a in (*held, prev_direction)] + [dma((4,)), dma((3,))],
        compiler_params=pltpu.CompilerParams(vmem_limit_bytes=VMEM_BYTES),
    )(*held)


def solution(mesh):
    in_specs = (
        P("gz", ("grp", "gx"), "gy"),
        P(None, "gz", ("grp", "gx"), "gy"),
        P(("grp", "gx"), "gy"),
        P(("grp", "gx"), "gy"),
        P(("grp", "gx"), "gy", None),
        P(("grp", "gx"), "gy", None),
        P(("grp", "gx"), "gy", None),
        P(("grp", "gx"), "gy", None),
        P("gz", ("grp", "gx"), "gy"),
        P("gz", ("grp", "gx"), "gy"),
    )
    out_specs = (
        P("gz", ("grp", "gx"), "gy"),
        P("gz", ("grp", "gx"), "gy"),
        P(None, ("grp", "gx"), "gy"),
    )
    return jax.shard_map(shards, mesh=mesh, in_specs=in_specs, out_specs=out_specs, check_vma=False)
```
